128 devices in a mesh: row: 8 (over y_hi, x), col: 16 (over z, y_lo, core).
Axes of the slice: x: 4, y: 4 (y_hi: 2, y_lo: 2; y = y_hi * 2 + y_lo), z: 4, core: 2. Of those that a mesh axis runs over, the one named last changes fastest.
Arguments:
- vectors: bfloat16 [64, 262144], P(None, ('col', 'row')), may hold values from -6 to 6
- blocks: bfloat16 [8, 8192, 128, 128], P('row', 'col'), may hold values from -0.125 to 0.125
- block_rows: int32 [8, 8192], P('row', 'col'), may hold values from 0 to 255, as said below
- block_cols: int32 [8, 8192], P('row', 'col'), may hold values from 0 to 127, as said below
- counts: int32 [8, 16], P('row', 'col'), may hold values from 1 to 512, as said below
Outputs:
- result: float32 [64, 262144], P(None, ('row', 'col'))
The draws below stay inside these ranges and needn't reach their ends.
Inputs may be any that keep to these rules, and one draw needn't show every extreme that they name: Within one owner pair the slots below its count name distinct positions (block_rows, block_cols) of its 256 x 256/2 grid of blocks; later slots hold 0. `block_cols`: see block_rows. `counts`: some owner pair holds exactly 512 blocks, and some other exactly one.
All inputs are finite; a program needn't handle non-finite values.
Results may differ from the reference program's by a relative error of at most 0.0029.
Values may be sent and summed in bfloat16 or wider, within the bound.
A program may use at most 128 MiB of HBM per device.

```python
import jax
import jax.numpy as jnp
from jax import lax

BS = 128
K = 64
RB = 256
CAP = 512
N = 262144
N_ROW = 8
N_COL = 16


def block_pattern(key):
    devices = N_ROW * N_COL
    grid_cells = RB * (RB // 2)
    base_key = jax.random.fold_in(key, 7)
    key_perm, key_base, key_level, key_full, key_least = jax.random.split(base_key, 5)
    owner_keys = jax.random.split(key_perm, devices)
    positions = jax.vmap(lambda subkey: jax.random.permutation(subkey, grid_cells))(owner_keys)[:, :CAP]
    base_count = jax.random.randint(key_base, (N_ROW, N_COL), CAP // 8, CAP // 4 + 1)
    row_level = jax.random.randint(key_level, (N_ROW, 1), 0, 4)
    row_factor = jnp.where(row_level == 3, 4, jnp.where(row_level == 2, 2, 1))
    slot_counts = jnp.minimum(base_count * row_factor, CAP)
    fullest = jax.random.randint(key_full, (), 0, devices)
    least = (fullest + 1 + jax.random.randint(key_least, (), 0, devices - 1)) % devices
    owner_ids = jnp.arange(devices, dtype=jnp.int32).reshape(N_ROW, N_COL)
    slot_counts = jnp.where(owner_ids == fullest, CAP, slot_counts)
    slot_counts = jnp.where(owner_ids == least, 1, slot_counts).astype(jnp.int32)
    live_slots = jnp.arange(CAP, dtype=jnp.int32)[None, :] < slot_counts.reshape(devices, 1)
    positions = jnp.where(live_slots, positions, 0).astype(jnp.int32)
    row_ids = (positions // (RB // 2)).reshape(N_ROW, N_COL * CAP).astype(jnp.int32)
    col_ids = (positions % (RB // 2)).reshape(N_ROW, N_COL * CAP).astype(jnp.int32)
    return (row_ids, col_ids, slot_counts)


def draw_block_rows(key, part):
    return block_pattern(key)[0]


def draw_block_cols(key, part):
    return block_pattern(key)[1]


def draw_counts(key, part):
    return block_pattern(key)[2]


def steps_of(key, dims, cuts, low, high):
    factor_of = 1.0
    for axis_at, blocks in cuts:
        draws = jax.random.uniform(jax.random.fold_in(jax.random.fold_in(key, 6), axis_at), (blocks,), jnp.float32, low / len(cuts), high / len(cuts))
        factor_of = factor_of * jnp.repeat(jnp.exp(draws), dims[axis_at] // blocks).reshape((-1,) + (1,) * (len(dims) - 1 - axis_at))
    return factor_of


def scatter_about(rng, dims, deviation, limit, shards=(), kind=jnp.bfloat16):
    array = jax.random.normal(rng, dims, jnp.float32) * deviation
    if len(shards) > 0:
        array = steps_of(rng, dims, shards, -0.22, 0.18) * array
    return jnp.clip(array, min=-limit, max=limit).astype(kind)


def setup_inputs(seed: int = 0) -> dict:
    seeds = jax.random.split(jax.random.key(seed), 6)
    vectors = scatter_about(seeds[0], (K, N), 1.0, 6.0, ((1, 128),))
    blocks = scatter_about(seeds[1], (N_ROW, N_COL * CAP, BS, BS), (BS * CAP * N_COL // (2 * RB)) ** -0.5, 0.125, ((0, 8), (1, 16)))
    block_rows = draw_block_rows(jax.random.fold_in(seeds[5], 71), 0)
    block_cols = draw_block_cols(jax.random.fold_in(seeds[5], 71), 0)
    counts = draw_counts(jax.random.fold_in(seeds[5], 71), 0)
    return {"vectors": vectors, "blocks": blocks, "block_rows": block_rows, "block_cols": block_cols, "counts": counts}


def owner_part(vec_panel, owner_blocks, row_ids, col_ids, slot_count):
    vec_width = vec_panel.shape[0]
    vec_tiles = vec_panel.reshape(vec_width, RB // 2, BS)
    picked = jnp.take(vec_tiles, col_ids, axis=1).astype(jnp.float32)
    product = jnp.einsum("ksc,src->ksr", picked, owner_blocks.astype(jnp.float32), precision=lax.Precision.HIGHEST)
    live_slots = (jnp.arange(CAP, dtype=jnp.int32) < slot_count).astype(jnp.float32)
    product = product * live_slots[None, :, None]
    summed = jax.ops.segment_sum(jnp.moveaxis(product, 1, 0), row_ids, num_segments=RB)
    return jnp.moveaxis(summed, 0, 1).reshape(vec_width, RB * BS)


def apply_matrix(vectors, blocks, block_rows, block_cols, counts):
    group_width = RB * BS // 2
    all_blocks = blocks.reshape(N_ROW * N_COL, CAP, BS, BS)
    all_rows = block_rows.reshape(N_ROW * N_COL, CAP)
    all_cols = block_cols.reshape(N_ROW * N_COL, CAP)
    all_counts = counts.reshape(N_ROW * N_COL)

    def add_owner(running, owner):
        row_owner = owner // N_COL
        col_owner = owner % N_COL
        vec_panel = lax.dynamic_slice_in_dim(vectors, col_owner * group_width, group_width, 1)
        part = owner_part(vec_panel, all_blocks[owner], all_rows[owner], all_cols[owner], all_counts[owner])
        current = lax.dynamic_slice_in_dim(running, row_owner * (RB * BS), RB * BS, 1)
        return lax.dynamic_update_slice_in_dim(running, current + part, row_owner * (RB * BS), 1), None

    running = jnp.zeros((K, N), jnp.float32)
    running, _ = lax.scan(add_owner, running, jnp.arange(N_ROW * N_COL, dtype=jnp.int32))
    return running


def reference(vectors, blocks, block_rows, block_cols, counts):
    first = apply_matrix(vectors, blocks, block_rows, block_cols, counts).astype(jnp.bfloat16)
    return apply_matrix(first, blocks, block_rows, block_cols, counts)
```

```python
import functools

import jax
import jax.numpy as jnp
from jax import lax
from jax.experimental import pallas as pl
from jax.experimental.pallas import tpu as pltpu
from jax.sharding import PartitionSpec as P

MESH = pl.DeviceIdType.MESH
K, BS, SLOTS = 64, 128, 512
SHARD = 16
TOP = 32767.0
VM = pl.BlockSpec(memory_space=pltpu.VMEM)
SM = pl.BlockSpec(memory_space=pltpu.SMEM)
F32, BF16, I16 = jnp.float32, jnp.bfloat16, jnp.int16


def place():
    row, col = lax.axis_index("row"), lax.axis_index("col")
    return row, col


def row_peers(row, col):
    x, y = row % 4, row // 4
    right = (y * 4 + (x + 1) % 4, col)
    left = (y * 4 + (x + 3) % 4, col)
    across = ((1 - y) * 4 + x, col)
    return right, left, across


def col_peers(row, col):
    z, y, h = col // 4, (col // 2) % 2, col % 2
    at = lambda z, y, h: (row, z * 4 + y * 2 + h)
    return at((z + 1) % 4, y, h), at((z + 3) % 4, y, h), at(z, 1 - y, h), at(z, y, 1 - h)


def greet(peers):
    barrier = pltpu.get_barrier_semaphore()
    for peer in peers:
        pl.semaphore_signal(barrier, inc=1, device_id=peer, device_id_type=MESH)
    return barrier


class Gather:
    def __init__(self, panel, send, recv):
        self.panel, self.send, self.recv = panel, send, recv
        self.row, self.col = place()
        self.right, self.left, self.across = row_peers(self.row, self.col)
        self.sent = []

    def copy(self, way, origin, half):
        part = self.panel.at[pl.ds(origin * SHARD + half * 8, 8)]
        to = (self.right, self.left, self.across)[way]
        return pltpu.make_async_remote_copy(
            src_ref=part, dst_ref=part, send_sem=self.send.at[way, origin, half], recv_sem=self.recv.at[origin, half],
            device_id=to, device_id_type=MESH)

    def go(self, way, origin, half):
        c = self.copy(way, origin, half)
        c.start()
        self.sent.append(c)

    def got(self, origin, half):
        self.copy(0, origin, half).wait_recv()

    def spread(self, origin):
        self.go(0, origin, 0)
        self.go(1, origin, 1)
        self.go(0, origin, 1)
        self.go(1, origin, 0)

    def start(self):
        self.go(2, self.row, 0)
        self.go(2, self.row, 1)
        self.spread(self.row)

    def middle(self):
        ro, lo, ao = self.right[0], self.left[0], self.across[0]
        self.got(ao, 0)
        self.go(0, ao, 0)
        self.go(1, ao, 0)
        self.got(ao, 1)
        self.go(1, ao, 1)
        self.go(0, ao, 1)
        self.got(lo, 0)
        self.go(0, lo, 0)
        self.got(ro, 1)
        self.go(1, ro, 1)

    def end(self):
        y = self.row // 4
        flip = (1 - 2 * y) * 4
        ro, lo = self.right[0], self.left[0]
        oo = y * 4 + (self.row + 2) % 4
        self.got(lo + flip, 0)
        self.go(0, lo + flip, 0)
        self.got(ro + flip, 1)
        self.go(1, ro + flip, 1)
        for o, half in ((lo, 1), (ro, 0), (oo, 0), (oo, 1), (lo + flip, 1), (ro + flip, 0), (oo + flip, 0), (oo + flip, 1)):
            self.got(o, half)
        for c in self.sent:
            c.wait_send()


GATHER_SEMS = [pltpu.SemaphoreType.DMA((3, 8, 2)), pltpu.SemaphoreType.DMA((8, 2))]
LOADS = 16


def gather_kernel(vec_ref, blocks_ref, panel, turned, send, recv, load_sem):
    per = SLOTS // LOADS
    loads = [pltpu.make_async_copy(blocks_ref.at[0, pl.ds(i * per, per)], turned.at[pl.ds(i * per, per)], load_sem.at[i])
             for i in range(LOADS)]
    for c in loads:
        c.start()
    row, col = place()
    barrier = greet(row_peers(row, col))
    for t in range(SHARD):
        panel[row * SHARD + t] = vec_ref[:, t * BS:(t + 1) * BS]
    pl.semaphore_wait(barrier, 3)

    def turn(first, last):
        for i in range(first, last):
            loads[i].wait()

        def step(i, _):
            for u in range(8):
                turned[i * 8 + u] = turned[i * 8 + u].T
            return 0

        lax.fori_loop(first * per // 8, last * per // 8, step, 0)

    g = Gather(panel, send, recv)
    g.start()
    turn(0, LOADS // 2)
    g.middle()
    turn(LOADS // 2, LOADS)
    g.end()


def gather(vectors, blocks):
    return pl.pallas_call(
        gather_kernel,
        in_specs=[VM, pl.BlockSpec(memory_space=pltpu.HBM)],
        out_specs=[VM, VM],
        out_shape=[pltpu.VMEM((8 * SHARD, K, BS), BF16), pltpu.VMEM((SLOTS, BS, BS), BF16)],
        scratch_shapes=GATHER_SEMS + [pltpu.SemaphoreType.DMA((LOADS,))],
        compiler_params=pltpu.CompilerParams(collective_id=0, has_side_effects=True, vmem_limit_bytes=36 << 20),
    )(vectors, blocks)


UNROLL = 32


def product_kernel(rows_ref, cols_ref, count_ref, vec_ref, blocks_ref, acc):
    count = count_ref[0, 0]

    def clear(i, _):
        acc[pl.ds(i * 8, 8)] = jnp.zeros((8, K, BS), F32)
        return 0

    lax.fori_loop(0, 33, clear, 0)

    def group(i, _):
        first = i * UNROLL
        prods = [jnp.dot(vec_ref[cols_ref[0, first + u]], blocks_ref[first + u], preferred_element_type=F32)
                 for u in range(UNROLL)]
        for u in range(UNROLL):
            s = first + u
            r = jnp.where(s < count, rows_ref[0, s], 256)
            acc[r] += prods[u]
        return 0

    lax.fori_loop(0, (count + UNROLL - 1) // UNROLL, group, 0)


def product(rows, cols, count, panel, blocks):
    return pl.pallas_call(
        product_kernel,
        in_specs=[SM, SM, SM, VM, VM],
        out_specs=VM,
        out_shape=pltpu.VMEM((264, K, BS), F32),
        compiler_params=pltpu.CompilerParams(vmem_limit_bytes=6 << 20),
    )(rows, cols, count, panel, blocks)


def put(x, data, scale, i):
    m = jnp.maximum(jnp.max(jnp.abs(x), axis=0, keepdims=True), 1e-30)
    data[i] = lax.round(x * (TOP / m), lax.RoundingMethod.TO_NEAREST_EVEN).astype(jnp.int32).astype(I16)
    scale[pl.ds(i, 1)] = m * (1.0 / TOP)


def get(data, scale, i):
    return data[i].astype(jnp.int32).astype(F32) * scale[pl.ds(i, 1)]


def each(n, step, unroll=4):
    def body(i, _):
        for u in range(unroll):
            step(i * unroll + u)
        return 0

    lax.fori_loop(0, n // unroll, body, 0)


class Sum:
    def __init__(self, acc, core_s, core_sc, core_r, core_rc, z_s, z_sc, z_r, z_rc, y_s, y_sc, y_r, y_rc, kept, sems):
        self.acc, self.kept, self.sems = acc, kept, sems
        self.core = (core_s, core_sc, core_r, core_rc)
        self.z = (z_s, z_sc, z_r, z_rc)
        self.y = (y_s, y_sc, y_r, y_rc)
        self.row, self.col = place()
        self.right, self.left, self.beside, self.sibling = col_peers(self.row, self.col)
        z = self.col // 4
        self.dest = ((z + 2) % 4, (z + 1) % 4, (z + 3) % 4, z)
        self.sent = []

    def copies(self, bufs, at, sem, to):
        s, sc, r, rc = bufs
        return [
            pltpu.make_async_remote_copy(src_ref=a.at[at], dst_ref=b.at[at], send_sem=self.sems.at[w, 0, sem],
                                         recv_sem=self.sems.at[w, 1, sem], device_id=to, device_id_type=MESH)
            for w, (a, b) in enumerate(((s, r), (sc, rc)))]

    def go(self, *a):
        for c in self.copies(*a):
            c.start()
            self.sent.append(c)

    def got(self, *a):
        for c in self.copies(*a):
            c.wait_recv()

    def tile(self, k, batch, i, h):
        half, y, j = i // 8, (i // 4) % 2, i % 4
        return (self.dest[k] * 4 + y * 2 + h) * SHARD + batch * 8 + half * 4 + j

    def core_send(self, k, b):
        n = k * 2 + b
        s, sc = self.core[0].at[n], self.core[1].at[n]
        h = 1 - self.col % 2
        each(16, lambda i: put(self.acc[self.tile(k, b, i, h)], s, sc, i))
        self.go(self.core, n, n, self.sibling)

    def core_wait(self, k, b):
        n = k * 2 + b
        self.got(self.core, n, n, self.sibling)

    def own(self, k, b, i):
        n = k * 2 + b
        return self.acc[self.tile(k, b, i, self.col % 2)] + get(self.core[2].at[n], self.core[3].at[n], i)

    def z_send(self, k, b, half, piece, add=None):
        n = b * 6 + piece
        s, sc, r, rc = self.z

        def step(i):
            x = self.own(k, b, half * 8 + i)
            if add is not None:
                x = x + get(r.at[b * 6 + add], rc.at[b * 6 + add], i)
            put(x, s.at[n], sc.at[n], i)

        each(8, step)
        self.go(self.z, n, 8 + n, (self.right, self.left)[piece in (1, 4, 5)])

    def z_wait(self, b, piece):
        n = b * 6 + piece
        self.got(self.z, n, 8 + n, self.right)

    def z_own(self, b, half, y, j):
        _, _, r, rc = self.z
        i = y * 4 + j
        n = b * 6 + half
        return self.own(3, b, half * 8 + i) + get(r.at[n + 2], rc.at[n + 2], i) + get(r.at[n + 4], rc.at[n + 4], i)

    def y_send(self, b):
        y = (self.col // 2) % 2
        s, sc, _, _ = self.y
        each(8, lambda i: put(self.z_own(b, i // 4, 1 - y, i % 4), s.at[b], sc.at[b], i))
        self.go(self.y, b, 20 + b, self.beside)

        def keep(i):
            self.kept[b * 8 + i] = self.z_own(b, i // 4, y, i % 4)

        each(8, keep)

    def total(self, b, j):
        _, _, r, rc = self.y
        return self.kept[b * 8 + j] + get(r.at[b], rc.at[b], j)

    def run(self, finish):
        for b in range(2):
            for k in range(4):
                self.core_send(k, b)
        for b in range(2):
            self.core_wait(0, b)
            self.z_send(0, b, 0, 0)
            self.z_send(0, b, 1, 1)
            self.core_wait(1, b)
            self.z_send(1, b, 1, 3)
            self.core_wait(2, b)
            self.z_send(2, b, 0, 4)
        for b in range(2):
            self.z_wait(b, 0)
            self.z_send(1, b, 0, 2, add=0)
            self.z_wait(b, 1)
            self.z_send(2, b, 1, 5, add=1)
        for b in range(2):
            self.core_wait(3, b)
            for piece in (2, 3, 4, 5):
                self.z_wait(b, piece)
            self.y_send(b)
        for b in range(2):
            self.got(self.y, b, 20 + b, self.beside)
            finish(b)

    def drain(self):
        for c in self.sent:
            c.wait_send()


def both(*shape):
    data = pltpu.VMEM(shape + (K, BS), I16)
    scale = pltpu.VMEM(shape + (BS,), F32)
    return [data, scale, data, scale]


SUM_SCRATCH = both(8, 16) + both(12, 8) + both(2, 8) + [pltpu.VMEM((SHARD, K, BS), F32), pltpu.SemaphoreType.DMA((2, 2, 24))]
N_SUM = len(SUM_SCRATCH)


def middle_kernel(acc, panel, *refs):
    first, hand_s, hand_r, send, recv = refs[N_SUM:]
    row, col = place()
    group = 2 * row + col // 8

    def target(i):
        return (i, group)

    def source(i):
        return (col // 2, 8 * (col % 2) + i)

    same = (group == col).astype(jnp.int32)
    barrier = greet(col_peers(row, col) + row_peers(row, col))
    for i in range(8):
        @pl.when(jnp.logical_or(source(i)[0] != row, source(i)[1] != col))
        def _():
            pl.semaphore_signal(barrier, inc=1, device_id=source(i), device_id_type=MESH)
    pl.semaphore_wait(barrier, 15 - same)

    total = Sum(acc, *refs[:N_SUM])

    def hand(i):
        part = pl.ds(i * SHARD + (col % 8) * 2, 2)
        return pltpu.make_async_remote_copy(
            src_ref=first.at[pl.ds(2 * i, 2)], dst_ref=panel.at[part], send_sem=hand_s.at[i],
            recv_sem=hand_r.at[col % 8], device_id=target(i), device_id_type=MESH)

    def is_other(i, dev):
        return jnp.logical_or(dev[0] != row, dev[1] != col)

    def finish(b):
        def step(j):
            first[b * 8 + j] = total.total(b, j).astype(BF16)

        each(8, step)
        for i in range(b * 4, b * 4 + 4):
            @pl.when(is_other(i, target(i)))
            def _():
                hand(i).start()

            @pl.when(jnp.logical_not(is_other(i, target(i))))
            def _():
                panel[pl.ds(i * SHARD + (col % 8) * 2, 2)] = first[pl.ds(2 * i, 2)]

    total.run(finish)
    for i in range(8):
        @pl.when(is_other(i, source(i)))
        def _():
            part = panel.at[pl.ds(row * SHARD + i * 2, 2)]
            pltpu.make_async_remote_copy(
                src_ref=first.at[pl.ds(0, 2)], dst_ref=part, send_sem=hand_s.at[0], recv_sem=hand_r.at[i],
                device_id=source(i), device_id_type=MESH).wait_recv()
    g = Gather(panel, send, recv)
    g.start()
    g.middle()
    g.end()
    for i in range(8):
        @pl.when(is_other(i, target(i)))
        def _():
            hand(i).wait_send()
    total.drain()


def middle(acc):
    return pl.pallas_call(
        middle_kernel,
        in_specs=[VM],
        out_specs=VM,
        out_shape=pltpu.VMEM((8 * SHARD, K, BS), BF16),
        scratch_shapes=SUM_SCRATCH + [pltpu.VMEM((SHARD, K, BS), BF16), pltpu.SemaphoreType.DMA((8,)),
                                      pltpu.SemaphoreType.DMA((8,))] + GATHER_SEMS,
        compiler_params=pltpu.CompilerParams(collective_id=1, has_side_effects=True, vmem_limit_bytes=16 << 20),
    )(acc)


def last_kernel(acc, out, *refs):
    row, col = place()
    barrier = greet(col_peers(row, col))
    pl.semaphore_wait(barrier, 4)
    total = Sum(acc, *refs)

    def finish(b):
        for j in range(8):
            t = b * 8 + j
            out[:, t * BS:(t + 1) * BS] = total.total(b, j)

    total.run(finish)
    total.drain()


def last(acc):
    return pl.pallas_call(
        last_kernel,
        in_specs=[VM],
        out_specs=VM,
        out_shape=jax.ShapeDtypeStruct((K, SHARD * BS), F32),
        scratch_shapes=SUM_SCRATCH,
        compiler_params=pltpu.CompilerParams(collective_id=2, has_side_effects=True, vmem_limit_bytes=16 << 20),
    )(acc)


def shards(vectors, blocks, block_rows, block_cols, counts):
    panel, turned = gather(vectors, blocks)
    acc = product(block_rows, block_cols, counts, panel, turned)
    panel = middle(acc)
    m = block_cols
    where = ((m % SHARD) // 2) * SHARD + (m // SHARD) * 2 + m % 2
    acc = product(block_rows, where, counts, panel, turned)
    return last(acc)


def solution(mesh):
    in_specs = (
        P(None, ("col", "row")),
        P("row", "col", None, None),
        P("row", "col"),
        P("row", "col"),
        P("row", "col"),
    )
    return jax.shard_map(shards, mesh=mesh, in_specs=in_specs, out_specs=P(None, ("row", "col")), check_vma=False)
```

```python
import functools

import jax
import jax.numpy as jnp
from jax import lax
from jax.experimental import pallas as pl
from jax.experimental.pallas import tpu as pltpu
from jax.sharding import PartitionSpec as P

MESH = pl.DeviceIdType.MESH
K, BS, SLOTS = 64, 128, 512
SHARD = 16
TOP = 32767.0
VM = pl.BlockSpec(memory_space=pltpu.VMEM)
SM = pl.BlockSpec(memory_space=pltpu.SMEM)
F32, BF16, I16 = jnp.float32, jnp.bfloat16, jnp.int16


def place():
    row, col = lax.axis_index("row"), lax.axis_index("col")
    return row, col


def row_peers(row, col):
    x, y = row % 4, row // 4
    right = (y * 4 + (x + 1) % 4, col)
    left = (y * 4 + (x + 3) % 4, col)
    across = ((1 - y) * 4 + x, col)
    return right, left, across


def col_peers(row, col):
    z, y, h = col // 4, (col // 2) % 2, col % 2
    at = lambda z, y, h: (row, z * 4 + y * 2 + h)
    return at((z + 1) % 4, y, h), at((z + 3) % 4, y, h), at(z, 1 - y, h), at(z, y, 1 - h)


def greet(peers):
    barrier = pltpu.get_barrier_semaphore()
    for peer in peers:
        pl.semaphore_signal(barrier, inc=1, device_id=peer, device_id_type=MESH)
    return barrier


class Gather:
    def __init__(self, part, send, recv, unit, across_first):
        self.part, self.send, self.recv, self.unit, self.across_first = part, send, recv, unit, across_first
        self.row, self.col = place()
        self.peers = row_peers(self.row, self.col)
        right, left, across = (p[0] for p in self.peers)
        x, y = self.row % 4, self.row // 4
        flip = (1 - 2 * y) * 4
        self.r, self.l, self.o, self.a = right, left, y * 4 + (x + 2) % 4, across
        self.ar, self.al, self.ao = right + flip, left + flip, self.o + flip
        self.sent = []

    def copy(self, way, origin, half):
        part = self.part(origin, half)
        return pltpu.make_async_remote_copy(
            src_ref=part, dst_ref=part, send_sem=self.send.at[self.unit, way, origin, half],
            recv_sem=self.recv.at[self.unit, origin, half], device_id=self.peers[way], device_id_type=MESH)

    def go(self, origin, half, *ways):
        for way in ways:
            c = self.copy(way, origin, half)
            c.start()
            self.sent.append(c)

    def got(self, origin, half):
        self.copy(0, origin, half).wait_recv()

    def start(self):
        me = self.row
        if self.across_first:
            self.go(me, 0, 2, 0)
            self.go(me, 1, 2, 1)
            self.go(me, 1, 0)
            self.go(me, 0, 1)
        else:
            self.go(me, 0, 0)
            self.go(me, 1, 1)
            self.go(me, 1, 0, 2)
            self.go(me, 0, 1, 2)

    def pass_on(self):
        more = () if self.across_first else (2,)
        self.got(self.l, 0)
        self.go(self.l, 0, 0, *more)
        self.got(self.r, 1)
        self.go(self.r, 1, 1, *more)

    def second(self):
        if self.across_first:
            self.got(self.a, 0)
            self.go(self.a, 0, 0, 1)
            self.got(self.a, 1)
            self.go(self.a, 1, 1, 0)
        else:
            self.got(self.l, 1)
            self.go(self.l, 1, 2)
            self.got(self.r, 0)
            self.go(self.r, 0, 2)

    def third(self):
        if self.across_first:
            self.got(self.al, 0)
            self.go(self.al, 0, 0)
            self.got(self.ar, 1)
            self.go(self.ar, 1, 1)
        else:
            for half in range(2):
                self.got(self.o, half)
                self.go(self.o, half, 2)

    def end(self):
        if self.across_first:
            rest = ((self.l, 1), (self.r, 0), (self.o, 0), (self.o, 1), (self.al, 1), (self.ar, 0))
        else:
            rest = ((self.a, 0), (self.a, 1), (self.al, 0), (self.ar, 1), (self.al, 1), (self.ar, 0))
        for origin, half in rest + ((self.ao, 0), (self.ao, 1)):
            self.got(origin, half)

    def drain(self):
        for c in self.sent:
            c.wait_send()


def gather_sems(units):
    return [pltpu.SemaphoreType.DMA((units, 3, 8, 2)), pltpu.SemaphoreType.DMA((units, 8, 2))]


LOADS = 16


def gather_kernel(vec_ref, blocks_ref, panel, turned, send, recv, load_sem):
    per = SLOTS // LOADS
    loads = [pltpu.make_async_copy(blocks_ref.at[0, pl.ds(i * per, per)], turned.at[pl.ds(i * per, per)], load_sem.at[i])
             for i in range(LOADS)]
    for c in loads:
        c.start()
    row, col = place()
    barrier = greet(row_peers(row, col))
    for t in range(SHARD):
        panel[row * SHARD + t] = vec_ref[:, t * BS:(t + 1) * BS]
    pl.semaphore_wait(barrier, 3)

    def turn(first, last):
        for i in range(first, last):
            loads[i].wait()

        def step(i, _):
            for u in range(8):
                turned[i * 8 + u] = turned[i * 8 + u].T
            return 0

        lax.fori_loop(first * per // 8, last * per // 8, step, 0)

    g = [Gather(lambda origin, half, u=u: panel.at[pl.ds(origin * SHARD + u * 10 + half * (5 - 2 * u), 5 - 2 * u)], send, recv, u, u == 0)
         for u in range(2)]
    q = LOADS // 4
    stages = (Gather.start, Gather.pass_on, Gather.second, Gather.third)
    for i, stage in enumerate(stages):
        for u in g:
            stage(u)
        turn(i * q, (i + 1) * q)
    for u in g:
        u.end()
    for u in g:
        u.drain()


def gather(vectors, blocks):
    return pl.pallas_call(
        gather_kernel,
        in_specs=[VM, pl.BlockSpec(memory_space=pltpu.HBM)],
        out_specs=[VM, VM],
        out_shape=[pltpu.VMEM((8 * SHARD, K, BS), BF16), pltpu.VMEM((SLOTS, BS, BS), BF16)],
        scratch_shapes=gather_sems(2) + [pltpu.SemaphoreType.DMA((LOADS,))],
        compiler_params=pltpu.CompilerParams(collective_id=0, has_side_effects=True, vmem_limit_bytes=36 << 20),
    )(vectors, blocks)


UNROLL = 32


def product_kernel(rows_ref, cols_ref, count_ref, vec_ref, blocks_ref, acc):
    count = count_ref[0, 0]

    def clear(i, _):
        acc[pl.ds(i * 8, 8)] = jnp.zeros((8, K, BS), F32)
        return 0

    lax.fori_loop(0, 33, clear, 0)

    def group(i, _):
        first = i * UNROLL
        prods = [jnp.dot(vec_ref[cols_ref[0, first + u]], blocks_ref[first + u], preferred_element_type=F32)
                 for u in range(UNROLL)]
        for u in range(UNROLL):
            s = first + u
            r = jnp.where(s < count, rows_ref[0, s], 256)
            acc[r] += prods[u]
        return 0

    lax.fori_loop(0, (count + UNROLL - 1) // UNROLL, group, 0)


def product(rows, cols, count, panel, blocks):
    return pl.pallas_call(
        product_kernel,
        in_specs=[SM, SM, SM, VM, VM],
        out_specs=VM,
        out_shape=pltpu.VMEM((264, K, BS), F32),
        compiler_params=pltpu.CompilerParams(vmem_limit_bytes=6 << 20),
    )(rows, cols, count, panel, blocks)


def put(x, data, scale, i):
    m = jnp.maximum(jnp.max(jnp.abs(x), axis=0, keepdims=True), 1e-30)
    data[i] = lax.round(x * (TOP / m), lax.RoundingMethod.TO_NEAREST_EVEN).astype(jnp.int32).astype(I16)
    scale[pl.ds(i, 1)] = m * (1.0 / TOP)


def get(data, scale, i):
    return data[i].astype(jnp.int32).astype(F32) * scale[pl.ds(i, 1)]


def each(n, step):
    unroll = min(n, 4)

    def body(i, _):
        for u in range(unroll):
            step(i * unroll + u)
        return 0

    lax.fori_loop(0, n // unroll, body, 0)


class Sum:
    def __init__(self, rounds, acc, core_s, core_sc, core_r, core_rc, z_s, z_sc, z_r, z_rc, y_s, y_sc, y_r, y_rc, kept, sems):
        self.acc, self.kept, self.sems = acc, kept, sems
        self.rounds, self.t = rounds, SHARD // (2 * rounds)
        self.core = (core_s, core_sc, core_r, core_rc)
        self.z = (z_s, z_sc, z_r, z_rc)
        self.y = (y_s, y_sc, y_r, y_rc)
        self.row, self.col = place()
        self.right, self.left, self.beside, self.sibling = col_peers(self.row, self.col)
        z, y = self.col // 4, (self.col // 2) % 2
        self.dest = ((z + 2) % 4, (z + 1) % 4, (z + 3) % 4, z)
        self.ydest = (1 - y, y)
        self.sent = []

    def copies(self, bufs, n, m, size, sem, to):
        s, sc, r, rc = bufs
        pairs = ((s.at[n, m, pl.ds(0, size)], r.at[n, m, pl.ds(0, size)]), (sc.at[n, m], rc.at[n, m]))
        return [
            pltpu.make_async_remote_copy(src_ref=a, dst_ref=b, send_sem=self.sems.at[w, 0, sem],
                                         recv_sem=self.sems.at[w, 1, sem], device_id=to, device_id_type=MESH)
            for w, (a, b) in enumerate(pairs)]

    def go(self, *a):
        for c in self.copies(*a):
            c.start()
            self.sent.append(c)

    def got(self, *a):
        for c in self.copies(*a):
            c.wait_recv()

    def core_args(self, n, m):
        return self.core, n, m, 2 * self.t, n * 4 + m, self.sibling

    def z_args(self, n, p):
        to = self.left if p in (1, 4, 5) else self.right
        return self.z, n, p, self.t // (1 + n % 2), self.rounds * 8 + n * 6 + p, to

    def y_args(self, n, k):
        return self.y, n, k, self.t, self.rounds * 20 + n * 4 + k, self.beside

    def shard_tile(self, n, i):
        return self.rounds * ((n % 2) * self.t + i) + n // 2

    def tile(self, n, k, v, i, h):
        pick = lambda options, at: options[at] if isinstance(at, int) else self.choose(options, at)
        return (pick(self.dest, k) * 4 + pick(self.ydest, v) * 2 + h) * SHARD + self.shard_tile(n, i)

    def choose(self, options, at):
        out = options[-1]
        for o in range(len(options) - 1):
            out = jnp.where(at == o, options[o], out)
        return out

    def core_fill(self, n, m):
        s, sc = self.core[0].at[n, m], self.core[1].at[n, m]
        for w in range(2):
            k, v = (m, w) if n % 2 == 0 else (2 * (m % 2) + w, m // 2)
            each(self.t, lambda i: put(self.acc[self.tile(n, k, v, i, 1 - self.col % 2)], s, sc, w * self.t + i))

    def core_send(self, n, m):
        self.core_fill(n, m)
        self.go(*self.core_args(n, m))

    def core_wait(self, n, m):
        self.got(*self.core_args(n, m))

    def own(self, n, k, v, i):
        m, w = (k, v) if n % 2 == 0 else (v * 2 + k // 2, k % 2)
        return self.acc[self.tile(n, k, v, i, self.col % 2)] + get(self.core[2].at[n, m], self.core[3].at[n, m], w * self.t + i)

    def add(self, bufs, n, m, i):
        return get(bufs[2].at[n, m], bufs[3].at[n, m], i)

    def before_z(self, n, k, v, i):
        x = self.own(n, k, v, i)
        return x if n % 2 == 0 else x + self.add(self.y, n, k, i)

    def z_send(self, n, k, half, p, plus=None):
        vs = (0, 1) if n % 2 == 0 else (1,)
        s, sc = self.z[0].at[n, p], self.z[1].at[n, p]
        for w, v in enumerate(vs):
            def step(i):
                at = w * (self.t // 2) + i
                x = self.before_z(n, k, v, half * (self.t // 2) + i)
                if plus is not None:
                    x = x + self.add(self.z, n, plus, at)
                put(x, s, sc, at)

            each(self.t // 2, step)
        self.go(*self.z_args(n, p))

    def z_wait(self, n, *pieces):
        for p in pieces:
            self.got(*self.z_args(n, p))

    def after_z(self, n, v, half, i):
        at = (v if n % 2 == 0 else 0) * (self.t // 2) + i
        x = self.before_z(n, 3, v, half * (self.t // 2) + i)
        return x + self.add(self.z, n, 2 + half, at) + self.add(self.z, n, 4 + half, at)

    def ring_first(self, n):
        self.z_send(n, 0, 0, 0)
        self.z_send(n, 0, 1, 1)

    def ring_pass(self, n):
        self.z_wait(n, 0)
        self.z_send(n, 1, 0, 2, plus=0)
        self.z_wait(n, 1)
        self.z_send(n, 2, 1, 5, plus=1)

    EARLY = ((0, 0), (1, 0), (0, 1), (0, 2), (1, 1))

    def fill(self, g):
        for n, m in self.EARLY:
            self.core_fill(2 * g + n, m)

    def a(self, g, filled=False):
        for n, m in self.EARLY:
            if not filled:
                self.core_fill(2 * g + n, m)
            self.go(*self.core_args(2 * g + n, m))

    def b(self, g):
        n = 2 * g
        self.core_wait(n, 0)
        self.ring_first(n)
        self.core_wait(n + 1, 0)
        self.y_first(n + 1, 0)
        self.y_first(n + 1, 1)
        self.core_wait(n, 1)
        self.z_send(n, 1, 1, 3)
        self.core_wait(n, 2)
        self.z_send(n, 2, 0, 4)
        self.core_wait(n + 1, 1)
        self.y_first(n + 1, 2)
        self.y_first(n + 1, 3)

    def y_first(self, n, k):
        s, sc = self.y[0].at[n, k], self.y[1].at[n, k]
        each(self.t, lambda i: put(self.own(n, k, 0, i), s, sc, i))
        self.go(*self.y_args(n, k))

    def c(self, g):
        for n, m in ((1, 2), (0, 3), (1, 3)):
            self.core_send(2 * g + n, m)

    def d(self, g):
        self.ring_pass(2 * g)

    def e(self, g):
        n = 2 * g + 1
        self.core_wait(n, 2)
        self.got(*self.y_args(n, 0))
        self.ring_first(n)
        self.got(*self.y_args(n, 1))
        self.z_send(n, 1, 1, 3)
        self.core_wait(n, 3)
        self.got(*self.y_args(n, 2))
        self.z_send(n, 2, 0, 4)

    def f(self, g):
        n = 2 * g
        self.core_wait(n, 3)
        self.z_wait(n, 2, 3, 4, 5)
        s, sc = self.y[0].at[n, 0], self.y[1].at[n, 0]
        for half in range(2):
            each(self.t // 2, lambda i: put(self.after_z(n, 0, half, i), s, sc, half * (self.t // 2) + i))
        self.go(*self.y_args(n, 0))
        for half in range(2):
            def keep(i):
                self.kept[g * self.t + half * (self.t // 2) + i] = self.after_z(n, 1, half, i)

            each(self.t // 2, keep)

    def g(self, g):
        self.ring_pass(2 * g + 1)

    def h(self, g, finish):
        n = 2 * g
        self.got(*self.y_args(n, 0))
        for i in range(self.t):
            finish(self.shard_tile(n, i), self.kept[g * self.t + i] + self.add(self.y, n, 0, i))

    def i(self, g, finish):
        n = 2 * g + 1
        self.got(*self.y_args(n, 3))
        self.z_wait(n, 2, 3, 4, 5)
        for i in range(self.t):
            finish(self.shard_tile(n, i), self.after_z(n, 1, i // (self.t // 2), i % (self.t // 2)))

    def take(self, names, finish):
        for name in names:
            step, g = getattr(self, name[0]), int(name[1])
            if name == "a0":
                step(g, True)
            elif name[0] in "hi":
                step(g, finish)
            else:
                step(g)

    def drain(self):
        for c in self.sent:
            c.wait_send()


ONE_ROUND = ("a0", "b0", "c0", "d0", "e0", "f0", "g0", "h0", "i0")

def both(n, m, tiles):
    data = pltpu.VMEM((n, m, tiles, K, BS), I16)
    scale = pltpu.VMEM((n, m, max(tiles, 8), BS), F32)
    return [data, scale, data, scale]


def sum_scratch(rounds):
    t = SHARD // (2 * rounds)
    return both(2 * rounds, 4, 2 * t) + both(2 * rounds, 6, t) + both(2 * rounds, 4, t) + [
        pltpu.VMEM((rounds * t, K, BS), F32), pltpu.SemaphoreType.DMA((2, 2, rounds * 28))]


N_SUM = len(sum_scratch(1))


def middle_kernel(acc, panel, *refs):
    first, hand_s, hand_r, send, recv = refs[N_SUM:]
    row, col = place()
    group = 2 * row + col // 8

    def target(i):
        return (i, group)

    def source(i):
        return (col // 2, 8 * (col % 2) + i)

    def is_other(dev):
        return jnp.logical_or(dev[0] != row, dev[1] != col)

    barrier = greet(col_peers(row, col) + row_peers(row, col))
    total = Sum(1, acc, *refs[:N_SUM])
    for i in range(8):
        @pl.when(is_other(source(i)))
        def _():
            pl.semaphore_signal(barrier, inc=1, device_id=source(i), device_id_type=MESH)
    total.fill(0)
    pl.semaphore_wait(barrier, 15 - (group == col).astype(jnp.int32))

    def hand(i):
        return pltpu.make_async_remote_copy(
            src_ref=first.at[pl.ds(2 * i, 2)], dst_ref=panel.at[col % 8, i], send_sem=hand_s.at[i],
            recv_sem=hand_r.at[col % 8], device_id=target(i), device_id_type=MESH)

    def finish(j, x):
        first[j] = x.astype(BF16)
        if j % 2 == 1:
            i = j // 2

            @pl.when(is_other(target(i)))
            def _():
                hand(i).start()

            @pl.when(jnp.logical_not(is_other(target(i))))
            def _():
                panel[col % 8, i] = first[pl.ds(2 * i, 2)]

    total.take(ONE_ROUND, finish)
    for i in range(8):
        @pl.when(is_other(source(i)))
        def _():
            pltpu.make_async_remote_copy(
                src_ref=first.at[pl.ds(0, 2)], dst_ref=panel.at[i, row], send_sem=hand_s.at[0], recv_sem=hand_r.at[i],
                device_id=source(i), device_id_type=MESH).wait_recv()

    def part(first_of, origin, half):
        return panel.at[pl.ds(first_of[half], first_of[half + 1] - first_of[half]), origin]

    every = [Gather(functools.partial(part, (0, 3, 5)), send, recv, 0, True),
             Gather(functools.partial(part, (5, 7, 8)), send, recv, 1, False)]
    for stage in (Gather.start, Gather.pass_on, Gather.second, Gather.third):
        for u in every:
            stage(u)
    for u in every:
        u.end()
    for u in every:
        u.drain()
    for i in range(8):
        @pl.when(is_other(target(i)))
        def _():
            hand(i).wait_send()
    total.drain()


def middle(acc):
    panel = pl.pallas_call(
        middle_kernel,
        in_specs=[VM],
        out_specs=VM,
        out_shape=pltpu.VMEM((8, 8, 2, K, BS), BF16),
        scratch_shapes=sum_scratch(1) + [pltpu.VMEM((SHARD, K, BS), BF16), pltpu.SemaphoreType.DMA((8,)),
                                       pltpu.SemaphoreType.DMA((8,))] + gather_sems(2),
        compiler_params=pltpu.CompilerParams(collective_id=1, has_side_effects=True, vmem_limit_bytes=20 << 20),
    )(acc)
    return panel.reshape(8 * SHARD, K, BS)


def last_kernel(acc, out, *refs):
    row, col = place()
    barrier = greet(col_peers(row, col))
    total = Sum(1, acc, *refs)
    total.fill(0)
    pl.semaphore_wait(barrier, 4)

    def finish(j, x):
        out[:, j * BS:(j + 1) * BS] = x

    total.take(ONE_ROUND, finish)
    total.drain()


def last(acc):
    return pl.pallas_call(
        last_kernel,
        in_specs=[VM],
        out_specs=VM,
        out_shape=jax.ShapeDtypeStruct((K, SHARD * BS), F32),
        scratch_shapes=sum_scratch(1),
        compiler_params=pltpu.CompilerParams(collective_id=2, has_side_effects=True, vmem_limit_bytes=20 << 20),
    )(acc)


def shards(vectors, blocks, block_rows, block_cols, counts):
    panel, turned = gather(vectors, blocks)
    acc = product(block_rows, block_cols, counts, panel, turned)
    panel = middle(acc)
    acc = product(block_rows, block_cols, counts, panel, turned)
    return last(acc)


def solution(mesh):
    in_specs = (
        P(None, ("col", "row")),
        P("row", "col", None, None),
        P("row", "col"),
        P("row", "col"),
        P("row", "col"),
    )
    return jax.shard_map(shards, mesh=mesh, in_specs=in_specs, out_specs=P(None, ("row", "col")), check_vma=False)
```

```python
import functools

import jax
import jax.numpy as jnp
from jax import lax
from jax.experimental import pallas as pl
from jax.experimental.pallas import tpu as pltpu
from jax.sharding import PartitionSpec as P

MESH = pl.DeviceIdType.MESH
K, BS, SLOTS = 64, 128, 512
SHARD = 16
TOP = 32000.0
VM = pl.BlockSpec(memory_space=pltpu.VMEM)
SM = pl.BlockSpec(memory_space=pltpu.SMEM)
F32, BF16, I16 = jnp.float32, jnp.bfloat16, jnp.int16


def place():
    row, col = lax.axis_index("row"), lax.axis_index("col")
    return row, col


def row_peers(row, col):
    x, y = row % 4, row // 4
    right = (y * 4 + (x + 1) % 4, col)
    left = (y * 4 + (x + 3) % 4, col)
    across = ((1 - y) * 4 + x, col)
    return right, left, across


def col_peers(row, col):
    z, y, h = col // 4, (col // 2) % 2, col % 2
    at = lambda z, y, h: (row, z * 4 + y * 2 + h)
    return at((z + 1) % 4, y, h), at((z + 3) % 4, y, h), at(z, 1 - y, h), at(z, y, 1 - h)


def greet(peers):
    barrier = pltpu.get_barrier_semaphore()
    for peer in peers:
        pl.semaphore_signal(barrier, inc=1, device_id=peer, device_id_type=MESH)
    return barrier


class Gather:
    def __init__(self, part, send, recv, unit, across_first):
        self.part, self.send, self.recv, self.unit, self.across_first = part, send, recv, unit, across_first
        self.row, self.col = place()
        self.peers = row_peers(self.row, self.col)
        right, left, across = (p[0] for p in self.peers)
        x, y = self.row % 4, self.row // 4
        flip = (1 - 2 * y) * 4
        self.r, self.l, self.o, self.a = right, left, y * 4 + (x + 2) % 4, across
        self.ar, self.al, self.ao = right + flip, left + flip, self.o + flip
        self.sent = []

    def copy(self, way, origin, half):
        part = self.part(origin, half)
        return pltpu.make_async_remote_copy(
            src_ref=part, dst_ref=part, send_sem=self.send.at[self.unit, way, origin, half],
            recv_sem=self.recv.at[self.unit, origin, half], device_id=self.peers[way], device_id_type=MESH)

    def go(self, origin, half, *ways):
        for way in ways:
            c = self.copy(way, origin, half)
            c.start()
            self.sent.append(c)

    def got(self, origin, half):
        self.copy(0, origin, half).wait_recv()

    def start(self):
        me = self.row
        if self.across_first:
            self.go(me, 0, 2, 0)
            self.go(me, 1, 2, 1)
            self.go(me, 1, 0)
            self.go(me, 0, 1)
        else:
            self.go(me, 0, 0)
            self.go(me, 1, 1)
            self.go(me, 1, 0, 2)
            self.go(me, 0, 1, 2)

    def pass_on(self):
        more = () if self.across_first else (2,)
        self.got(self.l, 0)
        self.go(self.l, 0, 0, *more)
        self.got(self.r, 1)
        self.go(self.r, 1, 1, *more)

    def second(self):
        if self.across_first:
            self.got(self.a, 0)
            self.go(self.a, 0, 0, 1)
            self.got(self.a, 1)
            self.go(self.a, 1, 1, 0)
        else:
            self.got(self.l, 1)
            self.go(self.l, 1, 2)
            self.got(self.r, 0)
            self.go(self.r, 0, 2)

    def third(self):
        if self.across_first:
            self.got(self.al, 0)
            self.go(self.al, 0, 0)
            self.got(self.ar, 1)
            self.go(self.ar, 1, 1)
        else:
            for half in range(2):
                self.got(self.o, half)
                self.go(self.o, half, 2)

    def end(self):
        if self.across_first:
            rest = ((self.l, 1), (self.r, 0), (self.o, 0), (self.o, 1), (self.al, 1), (self.ar, 0))
        else:
            rest = ((self.a, 0), (self.a, 1), (self.al, 0), (self.ar, 1), (self.al, 1), (self.ar, 0))
        for origin, half in rest + ((self.ao, 0), (self.ao, 1)):
            self.got(origin, half)

    def drain(self):
        for c in self.sent:
            c.wait_send()


def gather_sems(units):
    return [pltpu.SemaphoreType.DMA((units, 3, 8, 2)), pltpu.SemaphoreType.DMA((units, 8, 2))]


LOADS = 16


def gather_kernel(vec_ref, blocks_ref, panel, turned, send, recv, load_sem):
    per = SLOTS // LOADS
    loads = [pltpu.make_async_copy(blocks_ref.at[0, pl.ds(i * per, per)], turned.at[pl.ds(i * per, per)], load_sem.at[i])
             for i in range(LOADS)]
    for c in loads:
        c.start()
    row, col = place()
    barrier = greet(row_peers(row, col))
    for t in range(SHARD):
        panel[row * SHARD + t] = vec_ref[:, t * BS:(t + 1) * BS]
    pl.semaphore_wait(barrier, 3)

    def turn(first, last):
        for i in range(first, last):
            loads[i].wait()

        def step(i, _):
            for u in range(8):
                turned[i * 8 + u] = turned[i * 8 + u].T
            return 0

        lax.fori_loop(first * per // 8, last * per // 8, step, 0)

    g = [Gather(lambda origin, half, u=u: panel.at[pl.ds(origin * SHARD + u * 10 + half * (5 - 2 * u), 5 - 2 * u)], send, recv, u, u == 0)
         for u in range(2)]
    q = LOADS // 4
    stages = (Gather.start, Gather.pass_on, Gather.second, Gather.third)
    for i, stage in enumerate(stages):
        for u in g:
            stage(u)
        turn(i * q, (i + 1) * q)
    for u in g:
        u.end()
    for u in g:
        u.drain()


def gather(vectors, blocks):
    return pl.pallas_call(
        gather_kernel,
        in_specs=[VM, pl.BlockSpec(memory_space=pltpu.HBM)],
        out_specs=[VM, VM],
        out_shape=[pltpu.VMEM((8 * SHARD, K, BS), BF16), pltpu.VMEM((SLOTS, BS, BS), BF16)],
        scratch_shapes=gather_sems(2) + [pltpu.SemaphoreType.DMA((LOADS,))],
        compiler_params=pltpu.CompilerParams(collective_id=0, has_side_effects=True, vmem_limit_bytes=36 << 20),
    )(vectors, blocks)


UNROLL = 128
LAG = 8


def product_kernel(rows_ref, cols_ref, count_ref, vec_ref, blocks_ref, acc):
    count = count_ref[0, 0]

    def clear(i, _):
        acc[pl.ds(i * 8, 8)] = jnp.zeros((8, K, BS), F32)
        return 0

    lax.fori_loop(0, 33, clear, 0)

    def group(i, _):
        first = i * UNROLL
        prods = {}
        for u in range(UNROLL + LAG):
            if u < UNROLL:
                prods[u] = jnp.dot(vec_ref[cols_ref[0, first + u]], blocks_ref[first + u], preferred_element_type=F32)
            if u >= LAG:
                s = first + u - LAG
                r = jnp.where(s < count, rows_ref[0, s], 256)
                acc[r] += prods.pop(u - LAG)
        return 0

    lax.fori_loop(0, (count + UNROLL - 1) // UNROLL, group, 0)


def product(rows, cols, count, panel, blocks):
    return pl.pallas_call(
        product_kernel,
        in_specs=[SM, SM, SM, VM, VM],
        out_specs=VM,
        out_shape=pltpu.VMEM((264, K, BS), F32),
        compiler_params=pltpu.CompilerParams(vmem_limit_bytes=6 << 20),
    )(rows, cols, count, panel, blocks)


def rows_of(i):
    return pl.ds(pl.multiple_of(i * K, K), K)


def put(x, data, power, i):
    m = jnp.maximum(jnp.max(jnp.abs(x), axis=0, keepdims=True), 1e-30)
    e = jnp.ceil(jnp.log2(m))
    q = lax.round(x * (jnp.exp2(-e) * TOP), lax.RoundingMethod.TO_NEAREST_EVEN)
    data[rows_of(i)] = q.astype(jnp.int32).astype(I16)
    power[pl.ds(i, 1)] = e


def get(data, scale, i):
    return data[rows_of(i)].astype(jnp.int32).astype(F32) * scale[pl.ds(i, 1)]


def each(n, step):
    unroll = min(n, 4)

    def body(i, _):
        for u in range(unroll):
            step(i * unroll + u)
        return 0

    lax.fori_loop(0, n // unroll, body, 0)


TAIL = 16


class Sum:
    def __init__(self, rounds, acc, core_s, core_sc, core_r, core_rc, z_s, z_sc, z_r, z_rc, y_s, y_sc, y_r, y_rc, kept, sems):
        self.acc, self.kept, self.sems = acc, kept, sems
        self.rounds, self.t = rounds, SHARD // (2 * rounds)
        self.core = (core_s, core_sc, core_r, core_rc)
        self.z = (z_s, z_sc, z_r, z_rc)
        self.y = (y_s, y_sc, y_r, y_rc)
        self.row, self.col = place()
        self.right, self.left, self.beside, self.sibling = col_peers(self.row, self.col)
        z, y = self.col // 4, (self.col // 2) % 2
        self.dest = ((z + 2) % 4, (z + 1) % 4, (z + 3) % 4, z)
        self.ydest = (1 - y, y)
        self.sent = []

    def clear(self):
        for bufs in (self.core, self.z, self.y):
            bufs[1][...] = jnp.zeros_like(bufs[1])

    def copy(self, bufs, n, m, size, sem, to):
        part = pl.ds(0, size * K + TAIL)
        return pltpu.make_async_remote_copy(
            src_ref=bufs[0].at[n, m, part], dst_ref=bufs[2].at[n, m, part], send_sem=self.sems.at[0, sem],
            recv_sem=self.sems.at[1, sem], device_id=to, device_id_type=MESH)

    def go(self, bufs, n, m, size, sem, to):
        bufs[0][n, m, pl.ds(size * K, TAIL)] = bufs[1][n, m].astype(jnp.int32).astype(I16)
        c = self.copy(bufs, n, m, size, sem, to)
        c.start()
        self.sent.append(c)

    def got(self, bufs, n, m, size, sem, to):
        self.copy(bufs, n, m, size, sem, to).wait_recv()
        powers = bufs[2][n, m, pl.ds(size * K, TAIL)].astype(jnp.int32).astype(F32)
        bufs[3][n, m] = jnp.exp2(powers) * (1.0 / TOP)

    def core_args(self, n, m):
        return self.core, n, m, 2 * self.t, n * 4 + m, self.sibling

    def z_args(self, n, p):
        to = self.left if p in (1, 4, 5) else self.right
        return self.z, n, p, self.t // (1 + n % 2), self.rounds * 8 + n * 6 + p, to

    def y_args(self, n, k):
        return self.y, n, k, self.t, self.rounds * 20 + n * 4 + k, self.beside

    def shard_tile(self, n, i):
        return self.rounds * ((n % 2) * self.t + i) + n // 2

    def tile(self, n, k, v, i, h):
        pick = lambda options, at: options[at] if isinstance(at, int) else self.choose(options, at)
        return (pick(self.dest, k) * 4 + pick(self.ydest, v) * 2 + h) * SHARD + self.shard_tile(n, i)

    def choose(self, options, at):
        out = options[-1]
        for o in range(len(options) - 1):
            out = jnp.where(at == o, options[o], out)
        return out

    def core_fill(self, n, m):
        s, sc = self.core[0].at[n, m], self.core[1].at[n, m]
        for w in range(2):
            k, v = (m, w) if n % 2 == 0 else (2 * (m % 2) + w, m // 2)
            each(self.t, lambda i: put(self.acc[self.tile(n, k, v, i, 1 - self.col % 2)], s, sc, w * self.t + i))

    def core_send(self, n, m):
        self.core_fill(n, m)
        self.go(*self.core_args(n, m))

    def core_wait(self, n, m):
        self.got(*self.core_args(n, m))

    def own(self, n, k, v, i):
        m, w = (k, v) if n % 2 == 0 else (v * 2 + k // 2, k % 2)
        return self.acc[self.tile(n, k, v, i, self.col % 2)] + get(self.core[2].at[n, m], self.core[3].at[n, m], w * self.t + i)

    def add(self, bufs, n, m, i):
        return get(bufs[2].at[n, m], bufs[3].at[n, m], i)

    def before_z(self, n, k, v, i):
        x = self.own(n, k, v, i)
        return x if n % 2 == 0 else x + self.add(self.y, n, k, i)

    def z_send(self, n, k, half, p, plus=None):
        vs = (0, 1) if n % 2 == 0 else (1,)
        s, sc = self.z[0].at[n, p], self.z[1].at[n, p]
        for w, v in enumerate(vs):
            def step(i):
                at = w * (self.t // 2) + i
                x = self.before_z(n, k, v, half * (self.t // 2) + i)
                if plus is not None:
                    x = x + self.add(self.z, n, plus, at)
                put(x, s, sc, at)

            each(self.t // 2, step)
        self.go(*self.z_args(n, p))

    def z_wait(self, n, *pieces):
        for p in pieces:
            self.got(*self.z_args(n, p))

    def after_z(self, n, v, half, i):
        at = (v if n % 2 == 0 else 0) * (self.t // 2) + i
        x = self.before_z(n, 3, v, half * (self.t // 2) + i)
        return x + self.add(self.z, n, 2 + half, at) + self.add(self.z, n, 4 + half, at)

    def ring_first(self, n):
        self.z_send(n, 0, 0, 0)
        self.z_send(n, 0, 1, 1)

    def ring_pass(self, n):
        self.z_wait(n, 0)
        self.z_send(n, 1, 0, 2, plus=0)
        self.z_wait(n, 1)
        self.z_send(n, 2, 1, 5, plus=1)

    EARLY = ((0, 0), (1, 0), (0, 1), (0, 2), (1, 1))

    def fill(self, g):
        for n, m in self.EARLY:
            self.core_fill(2 * g + n, m)

    def a(self, g, filled=False):
        for n, m in self.EARLY:
            if not filled:
                self.core_fill(2 * g + n, m)
            self.go(*self.core_args(2 * g + n, m))

    def b(self, g):
        n = 2 * g
        self.core_wait(n, 0)
        self.ring_first(n)
        self.core_wait(n + 1, 0)
        self.y_first(n + 1, 0)
        self.y_first(n + 1, 1)
        self.core_wait(n, 1)
        self.z_send(n, 1, 1, 3)
        self.core_wait(n, 2)
        self.z_send(n, 2, 0, 4)
        self.core_wait(n + 1, 1)
        self.y_first(n + 1, 2)
        self.y_first(n + 1, 3)

    def y_first(self, n, k):
        s, sc = self.y[0].at[n, k], self.y[1].at[n, k]
        each(self.t, lambda i: put(self.own(n, k, 0, i), s, sc, i))
        self.go(*self.y_args(n, k))

    def c(self, g):
        for n, m in ((1, 2), (0, 3), (1, 3)):
            self.core_send(2 * g + n, m)

    def d(self, g):
        self.ring_pass(2 * g)

    def e(self, g):
        n = 2 * g + 1
        self.core_wait(n, 2)
        self.got(*self.y_args(n, 0))
        self.ring_first(n)
        self.got(*self.y_args(n, 1))
        self.z_send(n, 1, 1, 3)
        self.core_wait(n, 3)
        self.got(*self.y_args(n, 2))
        self.z_send(n, 2, 0, 4)

    def f(self, g):
        n = 2 * g
        self.core_wait(n, 3)
        self.z_wait(n, 2, 3, 4, 5)
        s, sc = self.y[0].at[n, 0], self.y[1].at[n, 0]
        for half in range(2):
            each(self.t // 2, lambda i: put(self.after_z(n, 0, half, i), s, sc, half * (self.t // 2) + i))
        self.go(*self.y_args(n, 0))
        for half in range(2):
            def keep(i):
                self.kept[g * self.t + half * (self.t // 2) + i] = self.after_z(n, 1, half, i)

            each(self.t // 2, keep)

    def g(self, g):
        self.ring_pass(2 * g + 1)

    def h(self, g, finish):
        n = 2 * g
        self.got(*self.y_args(n, 0))
        for i in range(self.t):
            finish(self.shard_tile(n, i), self.kept[g * self.t + i] + self.add(self.y, n, 0, i))

    def i(self, g, finish):
        n = 2 * g + 1
        self.got(*self.y_args(n, 3))
        self.z_wait(n, 2, 3, 4, 5)
        for i in range(self.t):
            finish(self.shard_tile(n, i), self.after_z(n, 1, i // (self.t // 2), i % (self.t // 2)))

    def take(self, names, finish):
        for name in names:
            step, g = getattr(self, name[0]), int(name[1])
            if name == "a0":
                step(g, True)
            elif name[0] in "hi":
                step(g, finish)
            else:
                step(g)

    def drain(self):
        for c in self.sent:
            c.wait_send()


ONE_ROUND = ("a0", "b0", "c0", "d0", "e0", "f0", "g0", "h0", "i0")

def both(n, m, tiles):
    data = pltpu.VMEM((n, m, tiles * K + TAIL, BS), I16)
    scale = pltpu.VMEM((n, m, TAIL, BS), F32)
    return [data, scale, data, scale]


def sum_scratch(rounds):
    t = SHARD // (2 * rounds)
    return both(2 * rounds, 4, 2 * t) + both(2 * rounds, 6, t) + both(2 * rounds, 4, t) + [
        pltpu.VMEM((rounds * t, K, BS), F32), pltpu.SemaphoreType.DMA((2, rounds * 28))]


N_SUM = len(sum_scratch(1))


def middle_kernel(acc, panel, *refs):
    first, hand_s, hand_r, send, recv = refs[N_SUM:]
    row, col = place()
    group = 2 * row + col // 8

    def target(i):
        return (i, group)

    def source(i):
        return (col // 2, 8 * (col % 2) + i)

    def is_other(dev):
        return jnp.logical_or(dev[0] != row, dev[1] != col)

    barrier = greet(col_peers(row, col) + row_peers(row, col))
    total = Sum(1, acc, *refs[:N_SUM])
    for i in range(8):
        @pl.when(is_other(source(i)))
        def _():
            pl.semaphore_signal(barrier, inc=1, device_id=source(i), device_id_type=MESH)
    total.clear()
    total.fill(0)
    pl.semaphore_wait(barrier, 15 - (group == col).astype(jnp.int32))

    def hand(i):
        return pltpu.make_async_remote_copy(
            src_ref=first.at[pl.ds(2 * i, 2)], dst_ref=panel.at[col % 8, i], send_sem=hand_s.at[i],
            recv_sem=hand_r.at[col % 8], device_id=target(i), device_id_type=MESH)

    def finish(j, x):
        first[j] = x.astype(BF16)
        if j % 2 == 1:
            i = j // 2

            @pl.when(is_other(target(i)))
            def _():
                hand(i).start()

            @pl.when(jnp.logical_not(is_other(target(i))))
            def _():
                panel[col % 8, i] = first[pl.ds(2 * i, 2)]

    total.take(ONE_ROUND, finish)
    for i in range(8):
        @pl.when(is_other(source(i)))
        def _():
            pltpu.make_async_remote_copy(
                src_ref=first.at[pl.ds(0, 2)], dst_ref=panel.at[i, row], send_sem=hand_s.at[0], recv_sem=hand_r.at[i],
                device_id=source(i), device_id_type=MESH).wait_recv()

    def part(first_of, origin, half):
        return panel.at[pl.ds(first_of[half], first_of[half + 1] - first_of[half]), origin]

    every = [Gather(functools.partial(part, (0, 3, 5)), send, recv, 0, True),
             Gather(functools.partial(part, (5, 7, 8)), send, recv, 1, False)]
    for stage in (Gather.start, Gather.pass_on, Gather.second, Gather.third):
        for u in every:
            stage(u)
    for u in every:
        u.end()
    for u in every:
        u.drain()
    for i in range(8):
        @pl.when(is_other(target(i)))
        def _():
            hand(i).wait_send()
    total.drain()


def middle(acc):
    panel = pl.pallas_call(
        middle_kernel,
        in_specs=[VM],
        out_specs=VM,
        out_shape=pltpu.VMEM((8, 8, 2, K, BS), BF16),
        scratch_shapes=sum_scratch(1) + [pltpu.VMEM((SHARD, K, BS), BF16), pltpu.SemaphoreType.DMA((8,)),
                                       pltpu.SemaphoreType.DMA((8,))] + gather_sems(2),
        compiler_params=pltpu.CompilerParams(collective_id=1, has_side_effects=True, vmem_limit_bytes=20 << 20),
    )(acc)
    return panel.reshape(8 * SHARD, K, BS)


def last_kernel(acc, out, *refs):
    row, col = place()
    barrier = greet(col_peers(row, col))
    total = Sum(1, acc, *refs)
    total.clear()
    total.fill(0)
    pl.semaphore_wait(barrier, 4)

    def finish(j, x):
        out[:, j * BS:(j + 1) * BS] = x

    total.take(ONE_ROUND, finish)
    total.drain()


def last(acc):
    return pl.pallas_call(
        last_kernel,
        in_specs=[VM],
        out_specs=VM,
        out_shape=jax.ShapeDtypeStruct((K, SHARD * BS), F32),
        scratch_shapes=sum_scratch(1),
        compiler_params=pltpu.CompilerParams(collective_id=2, has_side_effects=True, vmem_limit_bytes=20 << 20),
    )(acc)


def shards(vectors, blocks, block_rows, block_cols, counts):
    panel, turned = gather(vectors, blocks)
    acc = product(block_rows, block_cols, counts, panel, turned)
    panel = middle(acc)
    acc = product(block_rows, block_cols, counts, panel, turned)
    return last(acc)


def solution(mesh):
    in_specs = (
        P(None, ("col", "row")),
        P("row", "col", None, None),
        P("row", "col"),
        P("row", "col"),
        P("row", "col"),
    )
    return jax.shard_map(shards, mesh=mesh, in_specs=in_specs, out_specs=P(None, ("row", "col")), check_vma=False)
```

```python
import functools

import jax
import jax.numpy as jnp
from jax import lax
from jax.experimental import pallas as pl
from jax.experimental.pallas import tpu as pltpu
from jax.sharding import PartitionSpec as P

MESH = pl.DeviceIdType.MESH
K, BS, SLOTS = 64, 128, 512
SHARD = 16
TOP = 32000.0
VM = pl.BlockSpec(memory_space=pltpu.VMEM)
SM = pl.BlockSpec(memory_space=pltpu.SMEM)
F32, BF16, I16 = jnp.float32, jnp.bfloat16, jnp.int16
ROWS = pltpu.VMEM((264, K, BS), F32)


def clear(ref):
    def step(i, _):
        ref[pl.ds(i * 8, 8)] = jnp.zeros((8, K, BS), F32)
        return 0

    lax.fori_loop(0, 33, step, 0)


def place():
    row, col = lax.axis_index("row"), lax.axis_index("col")
    return row, col


def row_peers(row, col):
    x, y = row % 4, row // 4
    right = (y * 4 + (x + 1) % 4, col)
    left = (y * 4 + (x + 3) % 4, col)
    across = ((1 - y) * 4 + x, col)
    return right, left, across


def col_peers(row, col):
    z, y, h = col // 4, (col // 2) % 2, col % 2
    at = lambda z, y, h: (row, z * 4 + y * 2 + h)
    return at((z + 1) % 4, y, h), at((z + 3) % 4, y, h), at(z, 1 - y, h), at(z, y, 1 - h)


def greet(peers):
    barrier = pltpu.get_barrier_semaphore()
    for peer in peers:
        pl.semaphore_signal(barrier, inc=1, device_id=peer, device_id_type=MESH)
    return barrier


class Gather:
    def __init__(self, part, send, recv, unit, across_first):
        self.part, self.send, self.recv, self.unit, self.across_first = part, send, recv, unit, across_first
        self.row, self.col = place()
        self.peers = row_peers(self.row, self.col)
        right, left, across = (p[0] for p in self.peers)
        x, y = self.row % 4, self.row // 4
        flip = (1 - 2 * y) * 4
        self.r, self.l, self.o, self.a = right, left, y * 4 + (x + 2) % 4, across
        self.ar, self.al, self.ao = right + flip, left + flip, self.o + flip
        self.sent = []

    def copy(self, way, origin, half):
        part = self.part(origin, half)
        return pltpu.make_async_remote_copy(
            src_ref=part, dst_ref=part, send_sem=self.send.at[self.unit, way, origin, half],
            recv_sem=self.recv.at[self.unit, origin, half], device_id=self.peers[way], device_id_type=MESH)

    def go(self, origin, half, *ways):
        for way in ways:
            c = self.copy(way, origin, half)
            c.start()
            self.sent.append(c)

    def got(self, origin, half):
        self.copy(0, origin, half).wait_recv()

    def start(self):
        me = self.row
        if self.across_first:
            self.go(me, 0, 2, 0)
            self.go(me, 1, 2, 1)
            self.go(me, 1, 0)
            self.go(me, 0, 1)
        else:
            self.go(me, 0, 0)
            self.go(me, 1, 1)
            self.go(me, 1, 0, 2)
            self.go(me, 0, 1, 2)

    def pass_on(self):
        more = () if self.across_first else (2,)
        self.got(self.l, 0)
        self.go(self.l, 0, 0, *more)
        self.got(self.r, 1)
        self.go(self.r, 1, 1, *more)

    def second(self):
        if self.across_first:
            self.got(self.a, 0)
            self.go(self.a, 0, 0, 1)
            self.got(self.a, 1)
            self.go(self.a, 1, 1, 0)
        else:
            self.got(self.l, 1)
            self.go(self.l, 1, 2)
            self.got(self.r, 0)
            self.go(self.r, 0, 2)

    def third(self):
        if self.across_first:
            self.got(self.al, 0)
            self.go(self.al, 0, 0)
            self.got(self.ar, 1)
            self.go(self.ar, 1, 1)
        else:
            for half in range(2):
                self.got(self.o, half)
                self.go(self.o, half, 2)

    def end(self):
        if self.across_first:
            rest = ((self.l, 1), (self.r, 0), (self.o, 0), (self.o, 1), (self.al, 1), (self.ar, 0))
        else:
            rest = ((self.a, 0), (self.a, 1), (self.al, 0), (self.ar, 1), (self.al, 1), (self.ar, 0))
        for origin, half in rest + ((self.ao, 0), (self.ao, 1)):
            self.got(origin, half)

    def drain(self):
        for c in self.sent:
            c.wait_send()


def gather_sems(units):
    return [pltpu.SemaphoreType.DMA((units, 3, 8, 2)), pltpu.SemaphoreType.DMA((units, 8, 2))]


LOADS = 16


def gather_kernel(vec_ref, blocks_ref, panel, turned, zeros, send, recv, load_sem):
    per = SLOTS // LOADS
    loads = [pltpu.make_async_copy(blocks_ref.at[0, pl.ds(i * per, per)], turned.at[pl.ds(i * per, per)], load_sem.at[i])
             for i in range(LOADS)]
    for c in loads:
        c.start()
    row, col = place()
    barrier = greet(row_peers(row, col))
    for t in range(SHARD):
        panel[row * SHARD + t] = vec_ref[:, t * BS:(t + 1) * BS]
    pl.semaphore_wait(barrier, 3)

    def turn(first, last):
        for i in range(first, last):
            loads[i].wait()

        def step(i, _):
            for u in range(8):
                turned[i * 8 + u] = turned[i * 8 + u].T
            return 0

        lax.fori_loop(first * per // 8, last * per // 8, step, 0)

    g = [Gather(lambda origin, half, u=u: panel.at[pl.ds(origin * SHARD + u * 8 + half * (4 - 0 * u), 4 - 0 * u)], send, recv, u, u == 0)
         for u in range(2)]
    q = LOADS // 4
    stages = (Gather.start, Gather.pass_on, Gather.second, Gather.third)
    for i, stage in enumerate(stages):
        for u in g:
            stage(u)
        turn(i * q, (i + 1) * q)
    clear(zeros)
    for u in g:
        u.end()
    for u in g:
        u.drain()


def gather(vectors, blocks):
    return pl.pallas_call(
        gather_kernel,
        in_specs=[VM, pl.BlockSpec(memory_space=pltpu.HBM)],
        out_specs=[VM, VM, VM],
        out_shape=[pltpu.VMEM((8 * SHARD, K, BS), BF16), pltpu.VMEM((SLOTS, BS, BS), BF16), ROWS],
        scratch_shapes=gather_sems(2) + [pltpu.SemaphoreType.DMA((LOADS,))],
        compiler_params=pltpu.CompilerParams(collective_id=0, has_side_effects=True, vmem_limit_bytes=36 << 20),
    )(vectors, blocks)


UNROLL = 128
LAG = 8


def product_kernel(rows_ref, cols_ref, count_ref, vec_ref, blocks_ref, zeros_ref, acc):
    count = count_ref[0, 0]

    def group(i, _):
        first = i * UNROLL
        prods = {}
        for u in range(UNROLL + LAG):
            if u < UNROLL:
                prods[u] = jnp.dot(vec_ref[cols_ref[0, first + u]], blocks_ref[first + u], preferred_element_type=F32)
            if u >= LAG:
                s = first + u - LAG
                r = jnp.where(s < count, rows_ref[0, s], 256)
                acc[r] += prods.pop(u - LAG)
        return 0

    lax.fori_loop(0, (count + UNROLL - 1) // UNROLL, group, 0)


def product(rows, cols, count, panel, blocks, zeros):
    return pl.pallas_call(
        product_kernel,
        in_specs=[SM, SM, SM, VM, VM, VM],
        out_specs=VM,
        out_shape=ROWS,
        input_output_aliases={5: 0},
        compiler_params=pltpu.CompilerParams(vmem_limit_bytes=6 << 20),
    )(rows, cols, count, panel, blocks, zeros)


def rows_of(i):
    return pl.ds(pl.multiple_of(i * K, K), K)


def put(x, data, power, i):
    m = jnp.maximum(jnp.max(jnp.abs(x), axis=0, keepdims=True), 1e-30)
    e = jnp.ceil(jnp.log2(m))
    q = lax.round(x * (jnp.exp2(-e) * TOP), lax.RoundingMethod.TO_NEAREST_EVEN)
    data[rows_of(i)] = q.astype(jnp.int32).astype(I16)
    power[pl.ds(i, 1)] = e


def get(data, scale, i):
    return data[rows_of(i)].astype(jnp.int32).astype(F32) * scale[pl.ds(i, 1)]


def each(n, step):
    unroll = {9: 3, 10: 5, 6: 3}.get(n, n if n < 8 else 4)

    def body(i, _):
        for u in range(unroll):
            step(i * unroll + u)
        return 0

    lax.fori_loop(0, n // unroll, body, 0)


SIZES = (8, 8)
HALVES = tuple(((t + 1) // 2, t // 2) for t in SIZES)


class Sum:
    EARLY = ((1, 0), (0, 0), (0, 1), (1, 1), (0, 2))
    LATE = ((1, 2), (0, 3), (1, 3))

    def __init__(self, acc, core_s, core_sc, core_r, core_rc, z_s, z_sc, z_r, z_rc, y_s, y_sc, y_r, y_rc, kept, sems):
        self.acc, self.kept, self.sems = acc, kept, sems
        self.core = (core_s, core_sc, core_r, core_rc)
        self.z = (z_s, z_sc, z_r, z_rc)
        self.y = (y_s, y_sc, y_r, y_rc)
        self.row, self.col = place()
        self.right, self.left, self.beside, self.sibling = col_peers(self.row, self.col)
        z, y = self.col // 4, (self.col // 2) % 2
        self.dest = ((z + 2) % 4, (z + 1) % 4, (z + 3) % 4, z)
        self.ydest = (1 - y, y)
        self.sent = []

    def clear(self):
        for bufs in (self.core, self.z, self.y):
            bufs[1][...] = jnp.zeros_like(bufs[1])

    def copy(self, bufs, n, m, size, sem, to):
        part = pl.ds(0, size * K + bufs[1].shape[2])
        return pltpu.make_async_remote_copy(
            src_ref=bufs[0].at[n, m, part], dst_ref=bufs[2].at[n, m, part], send_sem=self.sems.at[0, sem],
            recv_sem=self.sems.at[1, sem], device_id=to, device_id_type=MESH)

    def go(self, bufs, n, m, size, sem, to):
        bufs[0][n, m, pl.ds(size * K, bufs[1].shape[2])] = bufs[1][n, m].astype(jnp.int32).astype(I16)
        c = self.copy(bufs, n, m, size, sem, to)
        c.start()
        self.sent.append(c)

    def got(self, bufs, n, m, size, sem, to):
        self.copy(bufs, n, m, size, sem, to).wait_recv()
        powers = bufs[2][n, m, pl.ds(size * K, bufs[1].shape[2])].astype(jnp.int32).astype(F32)
        bufs[3][n, m] = jnp.exp2(powers) * (1.0 / TOP)

    def core_args(self, n, m):
        return self.core, n, m, 2 * SIZES[n], n * 4 + m, self.sibling

    def z_args(self, n, p):
        to = self.left if p in (1, 4, 5) else self.right
        return self.z, n, p, HALVES[n][p % 2] * (2 - n), 8 + n * 6 + p, to

    def y_args(self, n, k):
        return self.y, n, k, SIZES[n], 20 + n * 4 + k, self.beside

    def tile(self, n, k, v, i, h):
        return (self.dest[k] * 4 + self.ydest[v] * 2 + h) * SHARD + n * SIZES[0] + i

    def core_fill(self, n, m):
        s, sc = self.core[0].at[n, m], self.core[1].at[n, m]
        for w in range(2):
            k, v = (m, w) if n == 0 else (2 * (m % 2) + w, m // 2)
            each(SIZES[n], lambda i: put(self.acc[self.tile(n, k, v, i, 1 - self.col % 2)], s, sc, w * SIZES[n] + i))

    def core_wait(self, n, m):
        self.got(*self.core_args(n, m))

    def own(self, n, k, v, i):
        m, w = (k, v) if n == 0 else (v * 2 + k // 2, k % 2)
        sibling = get(self.core[2].at[n, m], self.core[3].at[n, m], w * SIZES[n] + i)
        return self.acc[self.tile(n, k, v, i, self.col % 2)] + sibling

    def add(self, bufs, n, m, i):
        return get(bufs[2].at[n, m], bufs[3].at[n, m], i)

    def before_z(self, n, k, v, i):
        x = self.own(n, k, v, i)
        return x if n == 0 else x + self.add(self.y, n, k, i)

    def z_send(self, n, k, p, plus=None):
        half = p % 2
        size, start = HALVES[n][half], half * HALVES[n][0]
        s, sc = self.z[0].at[n, p], self.z[1].at[n, p]
        for w, v in enumerate((0, 1) if n == 0 else (1,)):
            def step(i):
                x = self.before_z(n, k, v, start + i)
                if plus is not None:
                    x = x + self.add(self.z, n, plus, w * size + i)
                put(x, s, sc, w * size + i)

            each(size, step)
        self.go(*self.z_args(n, p))

    def z_wait(self, n, *pieces):
        for p in pieces:
            self.got(*self.z_args(n, p))

    def after_z(self, n, v, half, i):
        at = (v if n == 0 else 0) * HALVES[n][half] + i
        x = self.before_z(n, 3, v, half * HALVES[n][0] + i)
        return x + self.add(self.z, n, 2 + half, at) + self.add(self.z, n, 4 + half, at)

    def ring_first(self, n):
        self.z_send(n, 0, 0)
        self.z_send(n, 0, 1)

    def ring_pass(self, n):
        self.z_wait(n, 0)
        self.z_send(n, 1, 2, plus=0)
        self.z_wait(n, 1)
        self.z_send(n, 2, 5, plus=1)

    def y_first(self, k):
        s, sc = self.y[0].at[1, k], self.y[1].at[1, k]
        each(SIZES[1], lambda i: put(self.own(1, k, 0, i), s, sc, i))
        self.go(*self.y_args(1, k))

    def fill(self):
        self.clear()
        for n, m in self.EARLY:
            self.core_fill(n, m)

    def run(self, finish):
        for n, m in self.EARLY:
            self.go(*self.core_args(n, m))
        self.core_wait(1, 0)
        self.y_first(0)
        self.core_wait(0, 0)
        self.ring_first(0)
        self.y_first(1)
        self.core_wait(0, 1)
        self.z_send(0, 1, 3)
        self.core_wait(1, 1)
        self.y_first(2)
        self.core_wait(0, 2)
        self.z_send(0, 2, 4)
        self.y_first(3)
        for n, m in self.LATE:
            self.core_fill(n, m)
            self.go(*self.core_args(n, m))
        self.ring_pass(0)
        self.core_wait(1, 2)
        self.got(*self.y_args(1, 0))
        self.ring_first(1)
        self.got(*self.y_args(1, 1))
        self.z_send(1, 1, 3)
        self.core_wait(1, 3)
        self.got(*self.y_args(1, 2))
        self.z_send(1, 2, 4)
        self.core_wait(0, 3)
        self.z_wait(0, 2, 3, 4, 5)
        s, sc = self.y[0].at[0, 0], self.y[1].at[0, 0]
        for half, size in enumerate(HALVES[0]):
            start = half * HALVES[0][0]
            each(size, lambda i: put(self.after_z(0, 0, half, i), s, sc, start + i))
        self.go(*self.y_args(0, 0))
        for half, size in enumerate(HALVES[0]):
            def keep(i):
                self.kept[half * HALVES[0][0] + i] = self.after_z(0, 1, half, i)

            each(size, keep)
        self.ring_pass(1)
        self.got(*self.y_args(0, 0))
        for i in range(SIZES[0]):
            finish(i, self.kept[i] + self.add(self.y, 0, 0, i))
        self.got(*self.y_args(1, 3))
        self.z_wait(1, 2, 3, 4, 5)
        for i in range(SIZES[1]):
            half = int(i >= HALVES[1][0])
            finish(SIZES[0] + i, self.after_z(1, 1, half, i - half * HALVES[1][0]))

    def drain(self):
        for c in self.sent:
            c.wait_send()


def both(n, m, tiles, tail=16):
    data = pltpu.VMEM((n, m, tiles * K + tail, BS), I16)
    scale = pltpu.VMEM((n, m, tail, BS), F32)
    return [data, scale, data, scale]


SUM_SCRATCH = both(2, 4, 2 * max(SIZES), 32) + both(2, 6, 2 * HALVES[0][0]) + both(2, 4, max(SIZES)) + [
    pltpu.VMEM((SIZES[0], K, BS), F32), pltpu.SemaphoreType.DMA((2, 28))]
N_SUM = len(SUM_SCRATCH)


def middle_kernel(acc, panel, zeros, *refs):
    first, hand_s, hand_r, send, recv = refs[N_SUM:]
    row, col = place()
    group = 2 * row + col // 8

    def target(i):
        return (i, group)

    def source(i):
        return (col // 2, 8 * (col % 2) + i)

    def is_other(dev):
        return jnp.logical_or(dev[0] != row, dev[1] != col)

    barrier = greet(col_peers(row, col) + row_peers(row, col))
    total = Sum(acc, *refs[:N_SUM])
    for i in range(8):
        @pl.when(is_other(source(i)))
        def _():
            pl.semaphore_signal(barrier, inc=1, device_id=source(i), device_id_type=MESH)
    total.fill()
    pl.semaphore_wait(barrier, 15 - (group == col).astype(jnp.int32))

    def hand(i):
        return pltpu.make_async_remote_copy(
            src_ref=first.at[pl.ds(2 * i, 2)], dst_ref=panel.at[col % 8, i], send_sem=hand_s.at[i],
            recv_sem=hand_r.at[col % 8], device_id=target(i), device_id_type=MESH)

    def finish(j, x):
        first[j] = x.astype(BF16)
        if j % 2 == 1:
            i = j // 2

            @pl.when(is_other(target(i)))
            def _():
                hand(i).start()

            @pl.when(jnp.logical_not(is_other(target(i))))
            def _():
                panel[col % 8, i] = first[pl.ds(2 * i, 2)]

    total.run(finish)
    for i in range(8):
        @pl.when(is_other(source(i)))
        def _():
            pltpu.make_async_remote_copy(
                src_ref=first.at[pl.ds(0, 2)], dst_ref=panel.at[i, row], send_sem=hand_s.at[0], recv_sem=hand_r.at[i],
                device_id=source(i), device_id_type=MESH).wait_recv()

    def part(first_of, origin, half):
        return panel.at[pl.ds(first_of[half], first_of[half + 1] - first_of[half]), origin]

    every = [Gather(functools.partial(part, (0, 2, 4)), send, recv, 0, True),
             Gather(functools.partial(part, (4, 6, 8)), send, recv, 1, False)]
    for stage in (Gather.start, Gather.pass_on, Gather.second, Gather.third):
        for u in every:
            stage(u)
    clear(zeros)
    for u in every:
        u.end()
    for u in every:
        u.drain()
    for i in range(8):
        @pl.when(is_other(target(i)))
        def _():
            hand(i).wait_send()
    total.drain()


def middle(acc):
    panel, zeros = pl.pallas_call(
        middle_kernel,
        in_specs=[VM],
        out_specs=[VM, VM],
        out_shape=[pltpu.VMEM((8, 8, 2, K, BS), BF16), ROWS],
        scratch_shapes=SUM_SCRATCH + [pltpu.VMEM((SHARD, K, BS), BF16), pltpu.SemaphoreType.DMA((8,)),
                                       pltpu.SemaphoreType.DMA((8,))] + gather_sems(2),
        compiler_params=pltpu.CompilerParams(collective_id=1, has_side_effects=True, vmem_limit_bytes=13 << 20),
    )(acc)
    return panel.reshape(8 * SHARD, K, BS), zeros


def last_kernel(acc, out, *refs):
    row, col = place()
    barrier = greet(col_peers(row, col))
    total = Sum(acc, *refs)
    total.fill()
    pl.semaphore_wait(barrier, 4)

    def finish(j, x):
        out[:, j * BS:(j + 1) * BS] = x

    total.run(finish)
    total.drain()


def last(acc):
    return pl.pallas_call(
        last_kernel,
        in_specs=[VM],
        out_specs=VM,
        out_shape=jax.ShapeDtypeStruct((K, SHARD * BS), F32),
        scratch_shapes=SUM_SCRATCH,
        compiler_params=pltpu.CompilerParams(collective_id=2, has_side_effects=True, vmem_limit_bytes=13 << 20),
    )(acc)


def shards(vectors, blocks, block_rows, block_cols, counts):
    panel, turned, zeros = gather(vectors, blocks)
    acc = product(block_rows, block_cols, counts, panel, turned, zeros)
    panel, zeros = middle(acc)
    acc = product(block_rows, block_cols, counts, panel, turned, zeros)
    return last(acc)


def solution(mesh):
    in_specs = (
        P(None, ("col", "row")),
        P("row", "col", None, None),
        P("row", "col"),
        P("row", "col"),
        P("row", "col"),
    )
    return jax.shard_map(shards, mesh=mesh, in_specs=in_specs, out_specs=P(None, ("row", "col")), check_vma=False)
```

```python
import functools

import jax
import jax.numpy as jnp
from jax import lax
from jax.experimental import pallas as pl
from jax.experimental.pallas import tpu as pltpu
from jax.sharding import PartitionSpec as P

MESH = pl.DeviceIdType.MESH
K, BS, SLOTS = 64, 128, 512
SHARD = 16
TOP = 32000.0
VM = pl.BlockSpec(memory_space=pltpu.VMEM)
SM = pl.BlockSpec(memory_space=pltpu.SMEM)
F32, BF16, I16 = jnp.float32, jnp.bfloat16, jnp.int16
ROWS = pltpu.VMEM((264, K, BS), F32)


def clear(ref):
    def step(i, _):
        ref[pl.ds(i * 8, 8)] = jnp.zeros((8, K, BS), F32)
        return 0

    lax.fori_loop(0, 33, step, 0)


def place():
    row, col = lax.axis_index("row"), lax.axis_index("col")
    return row, col


def row_peers(row, col):
    x, y = row % 4, row // 4
    right = (y * 4 + (x + 1) % 4, col)
    left = (y * 4 + (x + 3) % 4, col)
    across = ((1 - y) * 4 + x, col)
    return right, left, across


def col_peers(row, col):
    z, y, h = col // 4, (col // 2) % 2, col % 2
    at = lambda z, y, h: (row, z * 4 + y * 2 + h)
    return at((z + 1) % 4, y, h), at((z + 3) % 4, y, h), at(z, 1 - y, h), at(z, y, 1 - h)


def greet(peers):
    barrier = pltpu.get_barrier_semaphore()
    for peer in peers:
        pl.semaphore_signal(barrier, inc=1, device_id=peer, device_id_type=MESH)
    return barrier


class Gather:
    def __init__(self, part, send, recv, unit, across_first):
        self.part, self.send, self.recv, self.unit, self.across_first = part, send, recv, unit, across_first
        self.row, self.col = place()
        self.peers = row_peers(self.row, self.col)
        right, left, across = (p[0] for p in self.peers)
        x, y = self.row % 4, self.row // 4
        flip = (1 - 2 * y) * 4
        self.r, self.l, self.o, self.a = right, left, y * 4 + (x + 2) % 4, across
        self.ar, self.al, self.ao = right + flip, left + flip, self.o + flip
        self.sent = []

    def copy(self, way, origin, half):
        part = self.part(origin, half)
        return pltpu.make_async_remote_copy(
            src_ref=part, dst_ref=part, send_sem=self.send.at[self.unit, way, origin, half],
            recv_sem=self.recv.at[self.unit, origin, half], device_id=self.peers[way], device_id_type=MESH)

    def go(self, origin, half, *ways):
        for way in ways:
            c = self.copy(way, origin, half)
            c.start()
            self.sent.append(c)

    def got(self, origin, half):
        self.copy(0, origin, half).wait_recv()

    def start(self):
        me = self.row
        if self.across_first:
            self.go(me, 0, 2, 0)
            self.go(me, 1, 2, 1)
            self.go(me, 1, 0)
            self.go(me, 0, 1)
        else:
            self.go(me, 0, 0)
            self.go(me, 1, 1)
            self.go(me, 1, 0, 2)
            self.go(me, 0, 1, 2)

    def pass_on(self):
        more = () if self.across_first else (2,)
        self.got(self.l, 0)
        self.go(self.l, 0, 0, *more)
        self.got(self.r, 1)
        self.go(self.r, 1, 1, *more)

    def second(self):
        if self.across_first:
            self.got(self.a, 0)
            self.go(self.a, 0, 0, 1)
            self.got(self.a, 1)
            self.go(self.a, 1, 1, 0)
        else:
            self.got(self.l, 1)
            self.go(self.l, 1, 2)
            self.got(self.r, 0)
            self.go(self.r, 0, 2)

    def third(self):
        if self.across_first:
            self.got(self.al, 0)
            self.go(self.al, 0, 0)
            self.got(self.ar, 1)
            self.go(self.ar, 1, 1)
        else:
            for half in range(2):
                self.got(self.o, half)
                self.go(self.o, half, 2)

    def end(self):
        if self.across_first:
            rest = ((self.l, 1), (self.r, 0), (self.o, 0), (self.o, 1), (self.al, 1), (self.ar, 0))
        else:
            rest = ((self.a, 0), (self.a, 1), (self.al, 0), (self.ar, 1), (self.al, 1), (self.ar, 0))
        for origin, half in rest + ((self.ao, 0), (self.ao, 1)):
            self.got(origin, half)

    def drain(self):
        for c in self.sent:
            c.wait_send()


def gather_sems(units):
    return [pltpu.SemaphoreType.DMA((units, 3, 8, 2)), pltpu.SemaphoreType.DMA((units, 8, 2))]


LOADS = 16


def gather_kernel(vec_ref, blocks_ref, panel, turned, zeros, send, recv, load_sem):
    per = SLOTS // LOADS
    loads = [pltpu.make_async_copy(blocks_ref.at[0, pl.ds(i * per, per)], turned.at[pl.ds(i * per, per)], load_sem.at[i])
             for i in range(LOADS)]
    for c in loads:
        c.start()
    row, col = place()
    barrier = greet(row_peers(row, col))
    for t in range(SHARD):
        panel[row * SHARD + t] = vec_ref[:, t * BS:(t + 1) * BS]
    pl.semaphore_wait(barrier, 3)

    def turn(first, last):
        for i in range(first, last):
            loads[i].wait()

        def step(i, _):
            for u in range(8):
                turned[i * 8 + u] = turned[i * 8 + u].T
            return 0

        lax.fori_loop(first * per // 8, last * per // 8, step, 0)

    g = [Gather(lambda origin, half, u=u: panel.at[pl.ds(origin * SHARD + u * 8 + half * (4 - 0 * u), 4 - 0 * u)], send, recv, u, u == 0)
         for u in range(2)]
    q = LOADS // 4
    stages = (Gather.start, Gather.pass_on, Gather.second, Gather.third)
    for i, stage in enumerate(stages):
        for u in g:
            stage(u)
        turn(i * q, (i + 1) * q)
    clear(zeros)
    for u in g:
        u.end()
    for u in g:
        u.drain()


def gather(vectors, blocks):
    return pl.pallas_call(
        gather_kernel,
        in_specs=[VM, pl.BlockSpec(memory_space=pltpu.HBM)],
        out_specs=[VM, VM, VM],
        out_shape=[pltpu.VMEM((8 * SHARD, K, BS), BF16), pltpu.VMEM((SLOTS, BS, BS), BF16), ROWS],
        scratch_shapes=gather_sems(2) + [pltpu.SemaphoreType.DMA((LOADS,))],
        compiler_params=pltpu.CompilerParams(collective_id=0, has_side_effects=True, vmem_limit_bytes=36 << 20),
    )(vectors, blocks)


UNROLL = 128
LAG = 8


def product_kernel(rows_ref, cols_ref, count_ref, vec_ref, blocks_ref, zeros_ref, acc):
    count = count_ref[0, 0]

    def group(i, _):
        first = i * UNROLL
        prods = {}
        for u in range(UNROLL + LAG):
            if u < UNROLL:
                prods[u] = jnp.dot(vec_ref[cols_ref[0, first + u]], blocks_ref[first + u], preferred_element_type=F32)
            if u >= LAG:
                s = first + u - LAG
                r = jnp.where(s < count, rows_ref[0, s], 256)
                acc[r] += prods.pop(u - LAG)
        return 0

    lax.fori_loop(0, (count + UNROLL - 1) // UNROLL, group, 0)


def product(rows, cols, count, panel, blocks, zeros):
    return pl.pallas_call(
        product_kernel,
        in_specs=[SM, SM, SM, VM, VM, VM],
        out_specs=VM,
        out_shape=ROWS,
        input_output_aliases={5: 0},
        compiler_params=pltpu.CompilerParams(vmem_limit_bytes=6 << 20),
    )(rows, cols, count, panel, blocks, zeros)


def rows_of(i):
    return pl.ds(pl.multiple_of(i * K, K), K)


def put(x, data, power, i):
    m = jnp.maximum(jnp.max(jnp.abs(x), axis=0, keepdims=True), 1e-30)
    e = jnp.ceil(jnp.log2(m))
    q = lax.round(x * (jnp.exp2(-e) * TOP), lax.RoundingMethod.TO_NEAREST_EVEN)
    data[rows_of(i)] = q.astype(jnp.int32).astype(I16)
    power[pl.ds(i, 1)] = e


def get(data, scale, i):
    return data[rows_of(i)].astype(jnp.int32).astype(F32) * scale[pl.ds(i, 1)]


def each(n, step):
    unroll = {9: 3, 10: 5, 6: 3}.get(n, n if n < 8 else 4)

    def body(i, _):
        for u in range(unroll):
            step(i * unroll + u)
        return 0

    lax.fori_loop(0, n // unroll, body, 0)


SIZES = (8, 8)
HALVES = tuple(((t + 1) // 2, t // 2) for t in SIZES)


class Sum:
    EARLY = ((1, 0), (0, 0), (0, 1), (1, 1), (0, 2))
    LATE = ((1, 2), (0, 3), (1, 3))

    def __init__(self, acc, core_s, core_sc, core_r, core_rc, z_s, z_sc, z_r, z_rc, y_s, y_sc, y_r, y_rc, kept, sems):
        self.acc, self.kept, self.sems = acc, kept, sems
        self.core = (core_s, core_sc, core_r, core_rc)
        self.z = (z_s, z_sc, z_r, z_rc)
        self.y = (y_s, y_sc, y_r, y_rc)
        self.row, self.col = place()
        self.right, self.left, self.beside, self.sibling = col_peers(self.row, self.col)
        z, y = self.col // 4, (self.col // 2) % 2
        self.dest = ((z + 2) % 4, (z + 1) % 4, (z + 3) % 4, z)
        self.ydest = (1 - y, y)
        self.sent = []

    def clear(self):
        for bufs in (self.core, self.z, self.y):
            bufs[1][...] = jnp.zeros_like(bufs[1])

    def copy(self, bufs, n, m, size, sem, to):
        part = pl.ds(0, size * K + bufs[1].shape[2])
        return pltpu.make_async_remote_copy(
            src_ref=bufs[0].at[n, m, part], dst_ref=bufs[2].at[n, m, part], send_sem=self.sems.at[0, sem],
            recv_sem=self.sems.at[1, sem], device_id=to, device_id_type=MESH)

    def go(self, bufs, n, m, size, sem, to):
        bufs[0][n, m, pl.ds(size * K, bufs[1].shape[2])] = bufs[1][n, m].astype(jnp.int32).astype(I16)
        c = self.copy(bufs, n, m, size, sem, to)
        c.start()
        self.sent.append(c)

    def got(self, bufs, n, m, size, sem, to):
        self.copy(bufs, n, m, size, sem, to).wait_recv()
        powers = bufs[2][n, m, pl.ds(size * K, bufs[1].shape[2])].astype(jnp.int32).astype(F32)
        bufs[3][n, m] = jnp.exp2(powers) * (1.0 / TOP)

    def core_args(self, n, m):
        return self.core, n, m, 2 * SIZES[n], n * 4 + m, self.sibling

    def z_args(self, n, p):
        to = self.left if p in (1, 4, 5) else self.right
        return self.z, n, p, HALVES[n][p % 2] * (2 - n), 8 + n * 6 + p, to

    def y_args(self, n, k):
        return self.y, n, k, SIZES[n], 20 + n * 4 + k, self.beside

    def tile(self, n, k, v, i, h):
        return (self.dest[k] * 4 + self.ydest[v] * 2 + h) * SHARD + n * SIZES[0] + i

    def core_fill(self, n, m):
        s, sc = self.core[0].at[n, m], self.core[1].at[n, m]
        for w in range(2):
            k, v = (m, w) if n == 0 else (2 * (m % 2) + w, m // 2)
            each(SIZES[n], lambda i: put(self.acc[self.tile(n, k, v, i, 1 - self.col % 2)], s, sc, w * SIZES[n] + i))

    def core_wait(self, n, m):
        self.got(*self.core_args(n, m))

    def own(self, n, k, v, i):
        m, w = (k, v) if n == 0 else (v * 2 + k // 2, k % 2)
        sibling = get(self.core[2].at[n, m], self.core[3].at[n, m], w * SIZES[n] + i)
        return self.acc[self.tile(n, k, v, i, self.col % 2)] + sibling

    def add(self, bufs, n, m, i):
        return get(bufs[2].at[n, m], bufs[3].at[n, m], i)

    def before_z(self, n, k, v, i):
        x = self.own(n, k, v, i)
        return x if n == 0 else x + self.add(self.y, n, k, i)

    def z_send(self, n, k, p, plus=None):
        half = p % 2
        size, start = HALVES[n][half], half * HALVES[n][0]
        s, sc = self.z[0].at[n, p], self.z[1].at[n, p]
        for w, v in enumerate((0, 1) if n == 0 else (1,)):
            def step(i):
                x = self.before_z(n, k, v, start + i)
                if plus is not None:
                    x = x + self.add(self.z, n, plus, w * size + i)
                put(x, s, sc, w * size + i)

            each(size, step)
        self.go(*self.z_args(n, p))

    def z_wait(self, n, *pieces):
        for p in pieces:
            self.got(*self.z_args(n, p))

    def after_z(self, n, v, half, i):
        at = (v if n == 0 else 0) * HALVES[n][half] + i
        x = self.before_z(n, 3, v, half * HALVES[n][0] + i)
        return x + self.add(self.z, n, 2 + half, at) + self.add(self.z, n, 4 + half, at)

    def ring_first(self, n):
        self.z_send(n, 0, 0)
        self.z_send(n, 0, 1)

    def ring_pass(self, n):
        self.z_wait(n, 0)
        self.z_send(n, 1, 2, plus=0)
        self.z_wait(n, 1)
        self.z_send(n, 2, 5, plus=1)

    def y_first(self, k):
        s, sc = self.y[0].at[1, k], self.y[1].at[1, k]
        each(SIZES[1], lambda i: put(self.own(1, k, 0, i), s, sc, i))
        self.go(*self.y_args(1, k))

    def fill(self):
        self.clear()
        for n, m in self.EARLY:
            self.core_fill(n, m)

    def run(self, finish):
        for n, m in self.EARLY:
            self.go(*self.core_args(n, m))
        self.core_wait(1, 0)
        self.y_first(0)
        self.core_wait(0, 0)
        self.ring_first(0)
        self.y_first(1)
        self.core_wait(0, 1)
        self.z_send(0, 1, 3)
        self.core_wait(1, 1)
        self.y_first(2)
        self.core_wait(0, 2)
        self.z_send(0, 2, 4)
        self.y_first(3)
        for n, m in self.LATE:
            self.core_fill(n, m)
            self.go(*self.core_args(n, m))
        self.ring_pass(0)
        self.core_wait(1, 2)
        self.got(*self.y_args(1, 0))
        self.ring_first(1)
        self.got(*self.y_args(1, 1))
        self.z_send(1, 1, 3)
        self.core_wait(1, 3)
        self.got(*self.y_args(1, 2))
        self.z_send(1, 2, 4)
        self.core_wait(0, 3)
        self.z_wait(0, 2, 3, 4, 5)
        s, sc = self.y[0].at[0, 0], self.y[1].at[0, 0]
        for half, size in enumerate(HALVES[0]):
            start = half * HALVES[0][0]
            each(size, lambda i: put(self.after_z(0, 0, half, i), s, sc, start + i))
        self.go(*self.y_args(0, 0))
        for half, size in enumerate(HALVES[0]):
            def keep(i):
                self.kept[half * HALVES[0][0] + i] = self.after_z(0, 1, half, i)

            each(size, keep)
        self.ring_pass(1)
        self.got(*self.y_args(0, 0))
        for i in range(SIZES[0]):
            finish(i, self.kept[i] + self.add(self.y, 0, 0, i))
        self.got(*self.y_args(1, 3))
        self.z_wait(1, 2, 3, 4, 5)
        for i in range(SIZES[1]):
            half = int(i >= HALVES[1][0])
            finish(SIZES[0] + i, self.after_z(1, 1, half, i - half * HALVES[1][0]))

    def drain(self):
        for c in self.sent:
            c.wait_send()


def both(n, m, tiles, tail=16):
    data = pltpu.VMEM((n, m, tiles * K + tail, BS), I16)
    scale = pltpu.VMEM((n, m, tail, BS), F32)
    return [data, scale, data, scale]


SUM_SCRATCH = both(2, 4, 2 * max(SIZES), 32) + both(2, 6, 2 * HALVES[0][0]) + both(2, 4, max(SIZES)) + [
    pltpu.VMEM((SIZES[0], K, BS), F32), pltpu.SemaphoreType.DMA((2, 28))]
N_SUM = len(SUM_SCRATCH)


def middle_kernel(acc, panel, zeros, *refs):
    first, hand_s, hand_r, send, recv = refs[N_SUM:]
    row, col = place()
    group = 2 * row + col // 8

    def target(i):
        return (i, group)

    def source(i):
        return (col // 2, 8 * (col % 2) + i)

    def is_other(dev):
        return jnp.logical_or(dev[0] != row, dev[1] != col)

    barrier = greet(col_peers(row, col) + row_peers(row, col))
    total = Sum(acc, *refs[:N_SUM])
    for i in range(8):
        @pl.when(is_other(source(i)))
        def _():
            pl.semaphore_signal(barrier, inc=1, device_id=source(i), device_id_type=MESH)
    total.fill()
    pl.semaphore_wait(barrier, 15 - (group == col).astype(jnp.int32))

    def hand(i):
        return pltpu.make_async_remote_copy(
            src_ref=first.at[pl.ds(2 * i, 2)], dst_ref=panel.at[col % 8, i], send_sem=hand_s.at[i],
            recv_sem=hand_r.at[col % 8], device_id=target(i), device_id_type=MESH)

    def finish(j, x):
        first[j] = x.astype(BF16)
        if j % 2 == 1:
            i = j // 2

            @pl.when(is_other(target(i)))
            def _():
                hand(i).start()

            @pl.when(jnp.logical_not(is_other(target(i))))
            def _():
                panel[col % 8, i] = first[pl.ds(2 * i, 2)]

    total.run(finish)
    def part(first_of, origin, half):
        return panel.at[pl.ds(first_of[half], first_of[half + 1] - first_of[half]), origin]

    every = [Gather(functools.partial(part, (0, 2, 4)), send, recv, 0, True),
             Gather(functools.partial(part, (4, 6, 8)), send, recv, 1, False)]
    for n, unit in enumerate(every):
        for i in range(4 * n, 4 * n + 4):
            @pl.when(is_other(source(i)))
            def _():
                pltpu.make_async_remote_copy(
                    src_ref=first.at[pl.ds(0, 2)], dst_ref=panel.at[i, row], send_sem=hand_s.at[0], recv_sem=hand_r.at[i],
                    device_id=source(i), device_id_type=MESH).wait_recv()
        unit.start()
    for stage in (Gather.pass_on, Gather.second, Gather.third):
        for u in every:
            stage(u)
    clear(zeros)
    for u in every:
        u.end()
    for u in every:
        u.drain()
    for i in range(8):
        @pl.when(is_other(target(i)))
        def _():
            hand(i).wait_send()
    total.drain()


def middle(acc):
    panel, zeros = pl.pallas_call(
        middle_kernel,
        in_specs=[VM],
        out_specs=[VM, VM],
        out_shape=[pltpu.VMEM((8, 8, 2, K, BS), BF16), ROWS],
        scratch_shapes=SUM_SCRATCH + [pltpu.VMEM((SHARD, K, BS), BF16), pltpu.SemaphoreType.DMA((8,)),
                                       pltpu.SemaphoreType.DMA((8,))] + gather_sems(2),
        compiler_params=pltpu.CompilerParams(collective_id=1, has_side_effects=True, vmem_limit_bytes=13 << 20),
    )(acc)
    return panel.reshape(8 * SHARD, K, BS), zeros


def last_kernel(acc, out, *refs):
    row, col = place()
    barrier = greet(col_peers(row, col))
    total = Sum(acc, *refs)
    total.fill()
    pl.semaphore_wait(barrier, 4)

    def finish(j, x):
        out[:, j * BS:(j + 1) * BS] = x

    total.run(finish)
    total.drain()


def last(acc):
    return pl.pallas_call(
        last_kernel,
        in_specs=[VM],
        out_specs=VM,
        out_shape=jax.ShapeDtypeStruct((K, SHARD * BS), F32),
        scratch_shapes=SUM_SCRATCH,
        compiler_params=pltpu.CompilerParams(collective_id=2, has_side_effects=True, vmem_limit_bytes=13 << 20),
    )(acc)


def shards(vectors, blocks, block_rows, block_cols, counts):
    panel, turned, zeros = gather(vectors, blocks)
    acc = product(block_rows, block_cols, counts, panel, turned, zeros)
    panel, zeros = middle(acc)
    acc = product(block_rows, block_cols, counts, panel, turned, zeros)
    return last(acc)


def solution(mesh):
    in_specs = (
        P(None, ("col", "row")),
        P("row", "col", None, None),
        P("row", "col"),
        P("row", "col"),
        P("row", "col"),
    )
    return jax.shard_map(shards, mesh=mesh, in_specs=in_specs, out_specs=P(None, ("row", "col")), check_vma=False)
```
